256 devices in a mesh: dp: 16 (over y_lo, z), row: 4 (over x), col: 4 (over y_hi, core).
Axes of the slice: x: 4, y: 4 (y_hi: 2, y_lo: 2; y = y_hi * 2 + y_lo), z: 8, core: 2. Of those that a mesh axis runs over, the one named last changes fastest.
Arguments:
- activations: bfloat16 [32768, 2048], P(('dp', 'col'), 'row'), may hold values from -6 to 6
- cotangent: bfloat16 [32768, 16, 512], P(('dp', 'row'), None, 'col'), may hold values from -0.046875 to 0.046875
- weight: bfloat16 [2048, 8192], P('row', ('dp', 'col')), may hold values from -0.046875 to 0.046875
Outputs:
- orthonormal: bfloat16 [2048, 8192], P('row', ('dp', 'col'))
- weight_grad: float32 [2048, 8192], P('row', ('dp', 'col'))
The draws below stay inside these ranges and needn't reach their ends.
All inputs are finite; a program needn't handle non-finite values.
Results may differ from the reference program's by a relative error of at most 0.0051.
Values may be sent and summed in bfloat16 or wider, within the bound.
A program may use at most 128 MiB of HBM per device.

```python
import jax
import jax.numpy as jnp

DW = 2048
FW = 8192
ITERS = 2
TOKENS = 32768
N_DP = 16


def strengthened(values, key, source, target, parts, factor):
    owner, partner = [(jnp.arange(values.shape[position]) // (values.shape[position] // parts)).reshape([-1 if axis == position else 1 for axis in range(values.ndim)]) for position in (source, target)]
    chosen = jax.random.permutation(key, parts)[partner]
    strong = (owner == chosen) | (owner == (partner + parts // 2) % parts)
    return jnp.where(strong, factor * values, values)


def level_of(stream_key, shape, pieces, low, high):
    loudness, own = 1.0, jax.random.fold_in(stream_key, 6)
    for dim, parts in pieces:
        heights = jnp.exp(jax.random.uniform(jax.random.fold_in(own, dim), (parts,), jnp.float32, low / len(pieces), high / len(pieces)))
        loudness = loudness * jnp.repeat(heights, shape[dim] // parts).reshape([-1 if axis == dim else 1 for axis in range(len(shape))])
    return loudness


def normal_values(key, shape, spread, limit, shards=(), held_as=jnp.bfloat16):
    drawn = spread * jax.random.normal(key, shape, jnp.float32)
    if shards:
        drawn = drawn * level_of(key, shape, shards, -0.22, 0.18)
    return jnp.clip(drawn, -limit, limit).astype(held_as)


def gaussian_with(own_key, dims, spread, most, cuts, heavy, held_as=jnp.bfloat16):
    drawn = spread * jax.random.normal(own_key, dims, jnp.float32)
    if cuts:
        drawn = drawn * level_of(own_key, dims, cuts, -0.22, 0.18)
    return jnp.clip(strengthened(drawn, jax.random.fold_in(own_key, 3), *heavy), -most, most).astype(held_as)


def setup_inputs(seed: int = 0) -> dict:
    seeds = jax.random.split(jax.random.key(seed), 4)
    activations = normal_values(seeds[0], (TOKENS, DW), 1.0, 6.0, ((0, 64), (1, 4)))
    cotangent = gaussian_with(seeds[1], (TOKENS, N_DP, FW // N_DP), TOKENS ** -0.5, 0.046875, ((0, 64), (2, 4)), (0, 1, 16, 2.0))
    weight = normal_values(seeds[2], (DW, FW), (2 * FW) ** -0.5, 0.046875, ((0, 4), (1, 64)))
    return {"activations": activations, "cotangent": cotangent, "weight": weight}


def reference(activations, cotangent, weight):
    cot_flat = cotangent.reshape(cotangent.shape[0], cotangent.shape[1] * cotangent.shape[2])
    grad_full = jnp.dot(activations.T, cot_flat, preferred_element_type=jnp.float32).astype(jnp.bfloat16)
    iterate = weight
    stored = []
    for counter in range(ITERS):
        gram_full = jnp.dot(iterate, iterate.T, preferred_element_type=jnp.float32).astype(jnp.bfloat16)
        stored.append((iterate, gram_full))
        product = jnp.dot(gram_full, iterate, preferred_element_type=jnp.float32)
        iterate = (1.5 * iterate.astype(jnp.float32) - 0.5 * product).astype(jnp.bfloat16)
    upstream = grad_full
    result = upstream.astype(jnp.float32)
    for counter in reversed(range(ITERS)):
        previous, gram_full = stored[counter]
        symmetric = jnp.dot(upstream, previous.T, preferred_element_type=jnp.float32)
        symmetric = (symmetric + jnp.dot(previous, upstream.T, preferred_element_type=jnp.float32)).astype(jnp.bfloat16)
        summed = jnp.dot(gram_full, upstream, preferred_element_type=jnp.float32)
        summed = summed + jnp.dot(symmetric, previous, preferred_element_type=jnp.float32)
        result = 1.5 * upstream.astype(jnp.float32) - 0.5 * summed
        upstream = result.astype(jnp.bfloat16)
    return iterate, result
```

```python
import jax
import jax.numpy as jnp
from jax import lax
from jax.experimental import pallas as pl
from jax.experimental.pallas import tpu as pltpu
from jax.sharding import PartitionSpec as P

LOOKAHEAD = 4
PLACES = {
    "sym0": 3, "scatter0": 4, "gather0": 6, "swap0": 8, "product0": 9, "tile0": 11,
    "sym1": 14, "scatter1": 15, "gather1": 17, "swap1": 17,
}


def nt(first, second):
    return lax.dot_general(first, second, (((1,), (1,)), ((), ())), preferred_element_type=jnp.float32)


def nn(first, second):
    return jnp.dot(first, second, preferred_element_type=jnp.float32)


def kernel(
    a_ref, c_ref, w_ref, x_out, g_out,
    a_all, a_t, c_all, own_part, part_send, part_recv,
    own, other, half, cs_send, cs_recv, zs_send, zs_recv, gram, own_prod, ps_send, ps_recv,
    local_sem, a_ss, a_rs, c_ss, c_rs, p_ss, p_rs,
    o_ss, o_rs, q_ss, q_rs, cs_ss, cs_rs, zs_ss, zs_rs, ag_ss, ag_rs, fw_ss, fw_rs, ps_ss, ps_rs,
):
    d, x, c = lax.axis_index("dp"), lax.axis_index("row"), lax.axis_index("col")
    y_lo, z, y_hi, core = d // 8, d % 8, c // 2, c % 2
    y = y_hi * 2 + y_lo

    def dev(x2, y2, z2, core2):
        return ((y2 % 2) * 8 + z2, x2, (y2 // 2) * 2 + core2)

    left, right = dev((x + 3) % 4, y, z, core), dev((x + 1) % 4, y, z, core)
    sibling = dev(x, y, z, 1 - core)
    hops_y = [dev(x, (y + k) % 4, z, core) for k in range(1, 4)]
    hops_z = [dev(x, y, (z + k) % 8, core) for k in range(1, 8)]

    barrier = pltpu.get_barrier_semaphore()
    for target in [left, right, sibling] + hops_y:
        pl.semaphore_signal(barrier, inc=1, device_id=target)

    @pl.loop(1, 16)
    def _(k):
        pl.semaphore_signal(barrier, inc=1, device_id=((d + k) % 16, x, c))

    @pl.when(x != y)
    def _():
        for k in range(4):
            pl.semaphore_signal(barrier, inc=1, device_id=dev(y, k, z, core))

    def remote(src, dst, ss, rs, target):
        return pltpu.make_async_remote_copy(
            src_ref=src, dst_ref=dst, send_sem=ss, recv_sem=rs, device_id=target
        )

    c_rows = pl.ds(pl.multiple_of(x * 512, 512), 512)
    copy_c = pltpu.make_async_copy(c_ref, c_all.at[:, c_rows, :], local_sem.at[0])
    copy_c.start()
    my_cols = pl.ds(pl.multiple_of(y * 128, 128), 128)
    own[0, :, my_cols] = w_ref[...]
    pl.semaphore_wait(barrier, 24)

    def col_of(k):
        return pl.ds(pl.multiple_of(k * 128, 128), 128)

    def own_copy(k, hop):
        return remote(
            own.at[k, :, my_cols], own.at[k, :, my_cols], o_ss.at[k, hop], o_rs.at[k, y],
            dev(x, (y + hop) % 4, z, core),
        )

    def other_copy(k, hop):
        return remote(
            own.at[k, :, my_cols], other.at[k, :, my_cols], q_ss.at[k, hop], q_rs.at[k, y],
            dev((x + hop) % 4, x, z, core),
        )

    def send_tile(k):
        for hop in (2, 1, 3):
            other_copy(k, hop).start()
            own_copy(k, hop).start()

    def wait_tile(k):
        for hop in range(1, 4):
            source = (y + hop) % 4
            view = own.at[k, :, col_of(source)]
            remote(view, view, o_ss.at[k, hop], o_rs.at[k, source], sibling).wait_recv()

        @pl.when(x != y)
        def _():
            for source in range(4):
                view = other.at[k, :, col_of(source)]
                remote(view, view, q_ss.at[k, 0], q_rs.at[k, source], sibling).wait_recv()

        @pl.when(x == y)
        def _():
            other[k] = own[k]

    my_half = pl.multiple_of(core * 256, 256)
    its_half = pl.multiple_of((1 - core) * 256, 256)

    def swap_copy(k):
        return remote(cs_send.at[k], cs_recv.at[k], cs_ss.at[k], cs_rs.at[k], sibling)

    def sym(k, pairs):
        wait_tile(k)

        def block(rows):
            total = None
            for first, second in pairs:
                term = nt(own[first, rows, :], other[second])
                total = term if total is None else total + term
            return total

        cs_send[k] = block(pl.ds(its_half, 256)).astype(jnp.bfloat16)
        swap_copy(k).start()
        half[k] = block(pl.ds(my_half, 256))

    def scatter_copy(k, hop):
        target = (z + hop) % 8
        return remote(
            zs_send.at[k, target], zs_recv.at[k, z], zs_ss.at[k, hop], zs_rs.at[k, z],
            dev(x, y, target, core),
        )

    def scatter(k):
        swap_copy(k).wait_recv()
        total = half[k] + cs_recv[k].astype(jnp.float32)
        half[k] = total
        zs_send[k] = total.astype(jnp.bfloat16).reshape(8, 32, 512)
        for hop in (4, 3, 5, 2, 6, 1, 7):
            scatter_copy(k, hop).start()

    def piece_rows(owner):
        return pl.ds(pl.multiple_of(core * 256 + owner * 32, 32), 32)

    def gather_copy(k, hop):
        view = gram.at[k, piece_rows(z), :]
        return remote(view, view, ag_ss.at[k, hop], ag_rs.at[k, z], dev(x, y, (z + hop) % 8, core))

    def gather(k):
        total = half[k, pl.ds(pl.multiple_of(z * 32, 32), 32), :]
        for hop in range(1, 8):
            source = (z + hop) % 8
            view = zs_recv.at[k, source]
            remote(view, view, zs_ss.at[k, hop], zs_rs.at[k, source], sibling).wait_recv()
            total = total + zs_recv[k, source].astype(jnp.float32)
        gram[k, piece_rows(z), :] = total.astype(jnp.bfloat16)
        for hop in (4, 3, 5, 2, 6, 1, 7):
            gather_copy(k, hop).start()

    def half_copy(k):
        view = gram.at[k, pl.ds(my_half, 256), :]
        return remote(view, view, fw_ss.at[k], fw_rs.at[k], sibling)

    def swap(k):
        for hop in range(1, 8):
            source = (z + hop) % 8
            view = gram.at[k, piece_rows(source), :]
            remote(view, view, ag_ss.at[k, hop], ag_rs.at[k, source], sibling).wait_recv()
        half_copy(k).start()

    def product_copy(k, hop):
        target = (y + hop) % 4
        return remote(
            ps_send.at[k, target], ps_recv.at[k, y], ps_ss.at[k, hop], ps_rs.at[k, y],
            dev(x, target, z, core),
        )

    def product(k, pairs):
        view = gram.at[k, pl.ds(its_half, 256), :]
        remote(view, view, fw_ss.at[k], fw_rs.at[k], sibling).wait_recv()
        for hop in (2, 1, 3, 0):
            target = (y + hop) % 4
            cols = col_of(target)
            total = None
            for matrix, panel in pairs:
                term = nn(gram[matrix], other[panel, :, cols])
                total = term if total is None else total + term
            if hop:
                ps_send[k, target] = total.astype(jnp.bfloat16)
                product_copy(k, hop).start()
            else:
                own_prod[...] = total

    def result(k, tile):
        total = own_prod[...]
        for hop in range(1, 4):
            source = (y + hop) % 4
            view = ps_recv.at[k, source]
            remote(view, view, ps_ss.at[k, hop], ps_rs.at[k, source], sibling).wait_recv()
            total = total + ps_recv[k, source].astype(jnp.float32)
        return 1.5 * own[tile, :, my_cols].astype(jnp.float32) - 0.5 * total

    def finish_tile(k, tile, following):
        own[following, :, my_cols] = result(k, tile).astype(jnp.bfloat16)
        send_tile(following)

    far = dev(x, (y + 2) % 4, z, core)
    far_c = (c + 2) % 4
    a_far = remote(a_ref, a_all.at[c], a_ss.at[0], a_rs.at[c], far)
    a_sib = remote(a_ref, a_all.at[c], a_ss.at[1], a_rs.at[c], sibling)
    a_fwd = remote(a_all.at[far_c], a_all.at[far_c], a_ss.at[2], a_rs.at[far_c], sibling)
    sib_c = y_hi * 2 + 1 - core
    far_sib_c = (sib_c + 2) % 4

    def a_wait(block):
        view = a_all.at[block]
        remote(view, view, a_ss.at[0], a_rs.at[block], sibling).wait_recv()

    def put_transposed(block, ref):
        cols = pl.ds(pl.multiple_of(block * 512, 512), 512)
        a_t[:, cols] = ref[...].T

    def chunk(i):
        return (d + 1 + i) % 16

    def c_copy(i, way):
        view = c_all.at[chunk(i), c_rows, :]
        return remote(view, view, c_ss.at[i, way], c_rs.at[i, way], left if way else right)

    def rows_of(source):
        return pl.ds(pl.multiple_of(source * 512, 512), 512)

    def c_forward(i, way):
        source = (x + 3) % 4 if way == 0 else (x + 1) % 4
        view = c_all.at[chunk(i), rows_of(source), :]
        return remote(view, view, c_ss.at[i, 2], c_rs.at[i, 2], left if way else right)

    def c_wait(i, slot):
        view = c_all.at[chunk(i), rows_of(0), :]
        remote(view, view, c_ss.at[i, slot], c_rs.at[i, slot], sibling).wait_recv()

    def part_copy(i):
        a = chunk(i)
        return remote(part_send.at[a], part_recv.at[d], p_ss.at[a], p_rs.at[d], (a, x, c))

    send_tile(0)
    a_far.start()
    a_sib.start()
    copy_c.wait()
    for i in range(LOOKAHEAD):
        c_copy(i, 0).start()
        c_copy(i, 1).start()
    put_transposed(c, a_ref)
    a_wait(sib_c)
    put_transposed(sib_c, a_all.at[sib_c])

    stages = {
        "sym0": lambda: sym(0, [(0, 0)]),
        "scatter0": lambda: scatter(0),
        "gather0": lambda: gather(0),
        "swap0": lambda: swap(0),
        "product0": lambda: product(0, [(0, 0)]),
        "tile0": lambda: finish_tile(0, 0, 1),
        "sym1": lambda: sym(1, [(1, 1)]),
        "scatter1": lambda: scatter(1),
        "gather1": lambda: gather(1),
        "swap1": lambda: swap(1),
    }

    @pl.loop(0, 17)
    def _(i):
        @pl.when(i + LOOKAHEAD < 16)
        def _():
            c_copy(i + LOOKAHEAD, 0).start()
            c_copy(i + LOOKAHEAD, 1).start()

        @pl.when(i < 16)
        def _():
            c_wait(i, 0)
            c_wait(i, 1)

            @pl.when(i % 2 == 0)
            def _():
                c_forward(i, 0).start()

            @pl.when(i % 2 == 1)
            def _():
                c_forward(i, 1).start()

        @pl.when(i == 0)
        def _():
            a_wait(far_c)
            a_fwd.start()
            put_transposed(far_c, a_all.at[far_c])
            a_wait(far_sib_c)
            put_transposed(far_sib_c, a_all.at[far_sib_c])

        @pl.when(i > 0)
        def _():
            c_wait(i - 1, 2)
            a = chunk(i - 1)
            block = nn(a_t[...], c_all[a])

            @pl.when(i < 16)
            def _():
                part_send[a] = block.astype(jnp.bfloat16)
                part_copy(i - 1).start()

            @pl.when(i == 16)
            def _():
                own_part[...] = block

        for name, place in PLACES.items():
            if place < 17:
                @pl.when(i == place)
                def _(name=name):
                    stages[name]()

    for name, place in PLACES.items():
        if place >= 17:
            stages[name]()

    own_sum = own_part[...]

    @pl.loop(1, 16)
    def _(k):
        source = (d + k) % 16
        view = part_recv.at[source]
        remote(view, view, p_ss.at[source], p_rs.at[source], sibling).wait_recv()

    @pl.loop(0, 8)
    def _(m):
        rows = pl.ds(pl.multiple_of(m * 64, 64), 64)
        total = own_part[rows, :]
        for k in range(1, 16):
            total = total + part_recv[(d + k) % 16, rows, :].astype(jnp.float32)
        own[2, rows, my_cols] = total.astype(jnp.bfloat16)

    send_tile(2)
    product(1, [(1, 1)])
    x_out[...] = result(1, 1).astype(jnp.bfloat16)

    sym(2, [(2, 1), (1, 2)])
    scatter(2)
    gather(2)
    swap(2)
    product(2, [(1, 2), (2, 1)])
    finish_tile(2, 2, 3)
    sym(3, [(3, 0), (0, 3)])
    scatter(3)
    gather(3)
    swap(3)
    product(3, [(0, 3), (3, 0)])
    g_out[...] = result(3, 3)

    for copy in (a_far, a_sib, a_fwd):
        copy.wait_send()

    @pl.loop(0, 16)
    def _(i):
        c_copy(i, 0).wait_send()
        c_copy(i, 1).wait_send()
        c_forward(i, 0).wait_send()

    @pl.loop(0, 15)
    def _(i):
        part_copy(i).wait_send()

    @pl.loop(0, 4)
    def _(k):
        for hop in range(1, 4):
            own_copy(k, hop).wait_send()
            other_copy(k, hop).wait_send()
            product_copy(k, hop).wait_send()
        for hop in range(1, 8):
            scatter_copy(k, hop).wait_send()
            gather_copy(k, hop).wait_send()
        swap_copy(k).wait_send()
        half_copy(k).wait_send()


def body(activations, cotangent, weight):
    chunks = cotangent.transpose(1, 0, 2)
    bf16, f32 = jnp.bfloat16, jnp.float32
    sems = [
        (1,), (3,), (4,), (16, 3), (16, 3), (16,), (16,),
        (4, 4), (4, 4), (4, 4), (4, 4), (4,), (4,), (4, 8), (4, 8), (4, 8), (4, 8), (4,), (4,), (4, 4), (4, 4),
    ]
    buffers = [
        ((4, 512, 512), bf16), ((512, 2048), bf16), ((16, 2048, 128), bf16), ((512, 128), f32),
        ((16, 512, 128), bf16), ((16, 512, 128), bf16),
        ((4, 512, 512), bf16), ((4, 512, 512), bf16), ((4, 256, 512), f32), ((4, 256, 512), bf16),
        ((4, 256, 512), bf16), ((4, 8, 32, 512), bf16), ((4, 8, 32, 512), bf16), ((4, 512, 512), bf16),
        ((512, 128), f32), ((4, 4, 512, 128), bf16), ((4, 4, 512, 128), bf16),
    ]
    vmem = pl.BlockSpec(memory_space=pltpu.VMEM)
    return pl.pallas_call(
        kernel,
        out_shape=(jax.ShapeDtypeStruct((512, 128), bf16), jax.ShapeDtypeStruct((512, 128), f32)),
        in_specs=[vmem, pl.BlockSpec(memory_space=pl.ANY), vmem],
        out_specs=(vmem, vmem),
        scratch_shapes=[pltpu.VMEM(s, t) for s, t in buffers] + [pltpu.SemaphoreType.DMA(s) for s in sems],
        compiler_params=pltpu.CompilerParams(
            collective_id=0, has_side_effects=True, vmem_limit_bytes=56 * 2**20
        ),
    )(activations, chunks, weight)


def solution(mesh):
    placed = (P(("dp", "col"), "row"), P(("dp", "row"), None, "col"), P("row", ("dp", "col")))
    return jax.shard_map(
        body,
        mesh=mesh,
        in_specs=placed,
        out_specs=(P("row", ("dp", "col")), P("row", ("dp", "col"))),
        check_vma=False,
    )
```

```python
import jax
import jax.numpy as jnp
from jax import lax
from jax.experimental import pallas as pl
from jax.experimental.pallas import tpu as pltpu
from jax.sharding import PartitionSpec as P

LOOKAHEAD = 4
PLACES = {"sym0": 4, "scatter0": 6, "gather0": 8, "product0": 10, "tile0": 13, "sym1": 16}


def nt(first, second):
    return lax.dot_general(first, second, (((1,), (1,)), ((), ())), preferred_element_type=jnp.float32)


def nn(first, second):
    return jnp.dot(first, second, preferred_element_type=jnp.float32)


def kernel(
    a_ref, c_ref, w_ref, x_out, g_out,
    a_all, a_t, c_all, own_part, part_send, part_recv,
    own, other, half, cs_send, cs_recv, zs_send, zs_recv, gram, own_prod, ps_send, ps_recv,
    local_sem, a_ss, a_rs, c_ss, c_rs, p_ss, p_rs,
    o_ss, o_rs, q_ss, q_rs, cs_ss, cs_rs, zs_ss, zs_rs, ag_ss, ag_rs, fw_ss, fw_rs, ps_ss, ps_rs,
):
    d, x, c = lax.axis_index("dp"), lax.axis_index("row"), lax.axis_index("col")
    y_lo, z, y_hi, core = d // 8, d % 8, c // 2, c % 2
    y = y_hi * 2 + y_lo

    def dev(x2, y2, z2, core2):
        return ((y2 % 2) * 8 + z2, x2, (y2 // 2) * 2 + core2)

    left, right = dev((x + 3) % 4, y, z, core), dev((x + 1) % 4, y, z, core)
    sibling = dev(x, y, z, 1 - core)
    hops_y = [dev(x, (y + k) % 4, z, core) for k in range(1, 4)]
    hops_z = [dev(x, y, (z + k) % 8, core) for k in range(1, 8)]

    barrier = pltpu.get_barrier_semaphore()
    for target in [left, right, sibling] + hops_y:
        pl.semaphore_signal(barrier, inc=1, device_id=target)

    @pl.loop(1, 16)
    def _(k):
        pl.semaphore_signal(barrier, inc=1, device_id=((d + k) % 16, x, c))

    @pl.when(x != y)
    def _():
        for k in range(4):
            pl.semaphore_signal(barrier, inc=1, device_id=dev(y, k, z, core))

    def remote(src, dst, ss, rs, target):
        return pltpu.make_async_remote_copy(
            src_ref=src, dst_ref=dst, send_sem=ss, recv_sem=rs, device_id=target
        )

    c_rows = pl.ds(pl.multiple_of(x * 512, 512), 512)
    copy_c = pltpu.make_async_copy(c_ref, c_all.at[:, c_rows, :], local_sem.at[0])
    copy_c.start()
    my_cols = pl.ds(pl.multiple_of(y * 128, 128), 128)
    own[0, :, my_cols] = w_ref[...]

    def put_transposed(block, ref):
        cols = pl.ds(pl.multiple_of(block * 512, 512), 512)
        a_t[:, cols] = ref[...].T

    put_transposed(c, a_ref)
    pl.semaphore_wait(barrier, 24)

    def col_of(k):
        return pl.ds(pl.multiple_of(k * 128, 128), 128)

    def chunk_rows(j):
        return pl.ds(j * 256, 256)

    def core_rows(j, h):
        return pl.ds(pl.multiple_of(j * 256 + h * 128, 128), 128)

    def own_copy(k, j, hop):
        view = own.at[k, chunk_rows(j), my_cols]
        return remote(
            view, view, o_ss.at[k, j, hop], o_rs.at[k, j, y], dev(x, (y + hop) % 4, z, core)
        )

    def other_copy(k, j, hop):
        return remote(
            own.at[k, chunk_rows(j), my_cols], other.at[k, chunk_rows(j), my_cols],
            q_ss.at[k, j, hop], q_rs.at[k, j, y], dev((x + hop) % 4, x, z, core),
        )

    def send_tile(k, j):
        for hop in (2, 1, 3):
            other_copy(k, j, hop).start()
            own_copy(k, j, hop).start()

    def wait_own(k, j):
        for hop in range(1, 4):
            source = (y + hop) % 4
            view = own.at[k, chunk_rows(j), col_of(source)]
            remote(view, view, o_ss.at[k, j, hop], o_rs.at[k, j, source], sibling).wait_recv()

    def wait_tile(k):
        for j in range(2):
            wait_own(k, j)

        @pl.when(x != y)
        def _():
            for j in range(2):
                for source in range(4):
                    view = other.at[k, chunk_rows(j), col_of(source)]
                    remote(view, view, q_ss.at[k, j, 0], q_rs.at[k, j, source], sibling).wait_recv()

        @pl.when(x == y)
        def _():
            other[k] = own[k]

    def swap_copy(k, j):
        return remote(cs_send.at[k, j], cs_recv.at[k, j], cs_ss.at[k, j], cs_rs.at[k, j], sibling)

    def sym(k, pairs):
        wait_tile(k)

        def block(rows):
            total = None
            for first, second in pairs:
                term = nt(own[first, rows, :], other[second])
                total = term if total is None else total + term
            return total

        for j in range(2):
            cs_send[k, j] = block(core_rows(j, 1 - core)).astype(jnp.bfloat16)
            swap_copy(k, j).start()
        for j in range(2):
            half[k, j] = block(core_rows(j, core))

    def scatter_copy(k, j, hop):
        target = (z + hop) % 8
        return remote(
            zs_send.at[k, j, target], zs_recv.at[k, j, z], zs_ss.at[k, j, hop], zs_rs.at[k, j, z],
            dev(x, y, target, core),
        )

    def scatter(k):
        for j in range(2):
            swap_copy(k, j).wait_recv()
            total = half[k, j] + cs_recv[k, j].astype(jnp.float32)
            half[k, j] = total
            zs_send[k, j] = total.astype(jnp.bfloat16).reshape(8, 16, 512)
            for hop in (4, 3, 5, 2, 6, 1, 7):
                scatter_copy(k, j, hop).start()

    def piece_rows(j, owner):
        return pl.ds(pl.multiple_of(j * 256 + core * 128 + owner * 16, 16), 16)

    def gather_copy(k, j, hop):
        view = gram.at[k, piece_rows(j, z), :]
        return remote(
            view, view, ag_ss.at[k, j, hop], ag_rs.at[k, j, z], dev(x, y, (z + hop) % 8, core)
        )

    def gather(k):
        for j in range(2):
            total = half[k, j, pl.ds(pl.multiple_of(z * 16, 16), 16), :]
            for hop in range(1, 8):
                source = (z + hop) % 8
                view = zs_recv.at[k, j, source]
                remote(view, view, zs_ss.at[k, j, hop], zs_rs.at[k, j, source], sibling).wait_recv()
                total = total + zs_recv[k, j, source].astype(jnp.float32)
            gram[k, piece_rows(j, z), :] = total.astype(jnp.bfloat16)
            for hop in (4, 3, 5, 2, 6, 1, 7):
                gather_copy(k, j, hop).start()

    def half_copy(k, j):
        view = gram.at[k, core_rows(j, core), :]
        return remote(view, view, fw_ss.at[k, j], fw_rs.at[k, j], sibling)

    def swap(k, j):
        for hop in range(1, 8):
            source = (z + hop) % 8
            view = gram.at[k, piece_rows(j, source), :]
            remote(view, view, ag_ss.at[k, j, hop], ag_rs.at[k, j, source], sibling).wait_recv()
        half_copy(k, j).start()

    def product_copy(k, j, hop):
        target = (y + hop) % 4
        return remote(
            ps_send.at[k, target, chunk_rows(j)], ps_recv.at[k, y, chunk_rows(j)],
            ps_ss.at[k, j, hop], ps_rs.at[k, j, y], dev(x, target, z, core),
        )

    def product(k, j, pairs):
        view = gram.at[k, core_rows(j, 1 - core), :]
        remote(view, view, fw_ss.at[k, j], fw_rs.at[k, j], sibling).wait_recv()
        rows = chunk_rows(j)
        for hop in (2, 1, 3, 0):
            target = (y + hop) % 4
            cols = col_of(target)
            total = None
            for matrix, panel in pairs:
                term = nn(gram[matrix, rows, :], other[panel, :, cols])
                total = term if total is None else total + term
            if hop:
                ps_send[k, target, rows] = total.astype(jnp.bfloat16)
                product_copy(k, j, hop).start()
            else:
                own_prod[rows, :] = total

    def swap_product(k, pairs):
        for j in range(2):
            swap(k, j)
            product(k, j, pairs)

    def result(k, j, tile):
        rows = chunk_rows(j)
        total = own_prod[rows, :]
        for hop in range(1, 4):
            source = (y + hop) % 4
            view = ps_recv.at[k, source, rows]
            remote(view, view, ps_ss.at[k, j, hop], ps_rs.at[k, j, source], sibling).wait_recv()
            total = total + ps_recv[k, source, rows].astype(jnp.float32)
        return 1.5 * own[tile, rows, my_cols].astype(jnp.float32) - 0.5 * total

    def finish_tile(k, tile, following):
        for j in range(2):
            own[following, chunk_rows(j), my_cols] = result(k, j, tile).astype(jnp.bfloat16)
            send_tile(following, j)

    def drain(k):
        for j in range(2):
            for hop in range(1, 4):
                own_copy(k, j, hop).wait_send()
                other_copy(k, j, hop).wait_send()
                product_copy(k, j, hop).wait_send()
            for hop in range(1, 8):
                scatter_copy(k, j, hop).wait_send()
                gather_copy(k, j, hop).wait_send()
            swap_copy(k, j).wait_send()
            half_copy(k, j).wait_send()

    far = dev(x, (y + 2) % 4, z, core)
    far_c = (c + 2) % 4
    a_far = remote(a_ref, a_all.at[c], a_ss.at[0], a_rs.at[c], far)
    a_sib = remote(a_ref, a_all.at[c], a_ss.at[1], a_rs.at[c], sibling)
    a_fwd = remote(a_all.at[far_c], a_all.at[far_c], a_ss.at[2], a_rs.at[far_c], sibling)
    sib_c = y_hi * 2 + 1 - core
    far_sib_c = (sib_c + 2) % 4

    def a_wait(block):
        view = a_all.at[block]
        remote(view, view, a_ss.at[0], a_rs.at[block], sibling).wait_recv()

    def chunk(i):
        return (d + 1 + i) % 16

    def c_copy(i, way):
        view = c_all.at[chunk(i), c_rows, :]
        return remote(view, view, c_ss.at[i, way], c_rs.at[i, way], left if way else right)

    def rows_of(source):
        return pl.ds(pl.multiple_of(source * 512, 512), 512)

    def c_forward(i, way):
        source = (x + 3) % 4 if way == 0 else (x + 1) % 4
        view = c_all.at[chunk(i), rows_of(source), :]
        return remote(view, view, c_ss.at[i, 2], c_rs.at[i, 2], left if way else right)

    def c_wait(i, slot):
        view = c_all.at[chunk(i), rows_of(0), :]
        remote(view, view, c_ss.at[i, slot], c_rs.at[i, slot], sibling).wait_recv()

    def part_copy(i):
        a = chunk(i)
        return remote(part_send.at[a], part_recv.at[d], p_ss.at[a], p_rs.at[d], (a, x, c))

    send_tile(0, 0)
    send_tile(0, 1)
    a_far.start()
    a_sib.start()
    copy_c.wait()
    for i in range(LOOKAHEAD):
        c_copy(i, 0).start()
        c_copy(i, 1).start()
    a_wait(sib_c)
    put_transposed(sib_c, a_all.at[sib_c])

    stages = {
        "sym0": lambda: sym(0, [(0, 0)]),
        "scatter0": lambda: scatter(0),
        "gather0": lambda: gather(0),
        "product0": lambda: swap_product(0, [(0, 0)]),
        "tile0": lambda: finish_tile(0, 0, 1),
        "sym1": lambda: sym(1, [(1, 1)]),
    }

    @pl.loop(0, 17)
    def _(i):
        @pl.when(i + LOOKAHEAD < 16)
        def _():
            c_copy(i + LOOKAHEAD, 0).start()
            c_copy(i + LOOKAHEAD, 1).start()

        @pl.when(i < 16)
        def _():
            c_wait(i, 0)
            c_wait(i, 1)

            @pl.when(i % 2 == 0)
            def _():
                c_forward(i, 0).start()

            @pl.when(i % 2 == 1)
            def _():
                c_forward(i, 1).start()

        @pl.when(i == 0)
        def _():
            a_wait(far_c)
            a_fwd.start()
            put_transposed(far_c, a_all.at[far_c])
            a_wait(far_sib_c)
            put_transposed(far_sib_c, a_all.at[far_sib_c])

        @pl.when(i > 0)
        def _():
            c_wait(i - 1, 2)
            a = chunk(i - 1)
            block = nn(a_t[...], c_all[a])

            @pl.when(i < 16)
            def _():
                part_send[a] = block.astype(jnp.bfloat16)
                part_copy(i - 1).start()

            @pl.when(i == 16)
            def _():
                own_part[...] = block

        for name, place in PLACES.items():
            if place < 17:
                @pl.when(i == place)
                def _(name=name):
                    stages[name]()


    @pl.loop(1, 16)
    def _(k):
        source = (d + k) % 16
        view = part_recv.at[source]
        remote(view, view, p_ss.at[source], p_rs.at[source], sibling).wait_recv()

    @pl.loop(0, 8)
    def _(m):
        rows = pl.ds(pl.multiple_of(m * 64, 64), 64)
        total = own_part[rows, :]
        for k in range(1, 16):
            total = total + part_recv[(d + k) % 16, rows, :].astype(jnp.float32)
        own[2, rows, my_cols] = total.astype(jnp.bfloat16)

    send_tile(2, 0)
    send_tile(2, 1)
    scatter(1)
    for copy in (a_far, a_sib, a_fwd):
        copy.wait_send()

    @pl.loop(0, 16)
    def _(i):
        c_copy(i, 0).wait_send()
        c_copy(i, 1).wait_send()
        c_forward(i, 0).wait_send()

    @pl.loop(0, 15)
    def _(i):
        part_copy(i).wait_send()

    sym(2, [(2, 1), (1, 2)])
    gather(1)
    scatter(2)
    drain(0)
    swap_product(1, [(1, 1)])
    gather(2)
    for j in range(2):
        x_out[chunk_rows(j), :] = result(1, j, 1).astype(jnp.bfloat16)
    drain(1)
    swap_product(2, [(1, 2), (2, 1)])
    finish_tile(2, 2, 3)
    drain(2)
    sym(3, [(3, 0), (0, 3)])
    scatter(3)
    gather(3)
    swap_product(3, [(0, 3), (3, 0)])
    for j in range(2):
        g_out[chunk_rows(j), :] = result(3, j, 3)
    drain(3)


def body(activations, cotangent, weight):
    chunks = cotangent.transpose(1, 0, 2)
    bf16, f32 = jnp.bfloat16, jnp.float32
    sems = [
        (1,), (3,), (4,), (16, 3), (16, 3), (16,), (16,),
        (4, 2, 4), (4, 2, 4), (4, 2, 4), (4, 2, 4), (4, 2), (4, 2), (4, 2, 8), (4, 2, 8), (4, 2, 8), (4, 2, 8),
        (4, 2), (4, 2), (4, 2, 4), (4, 2, 4),
    ]
    buffers = [
        ((4, 512, 512), bf16), ((512, 2048), bf16), ((16, 2048, 128), bf16), ((512, 128), f32),
        ((16, 512, 128), bf16), ((16, 512, 128), bf16),
        ((4, 512, 512), bf16), ((4, 512, 512), bf16), ((4, 2, 128, 512), f32), ((4, 2, 128, 512), bf16),
        ((4, 2, 128, 512), bf16), ((4, 2, 8, 16, 512), bf16), ((4, 2, 8, 16, 512), bf16), ((4, 512, 512), bf16),
        ((512, 128), f32), ((4, 4, 512, 128), bf16), ((4, 4, 512, 128), bf16),
    ]
    vmem = pl.BlockSpec(memory_space=pltpu.VMEM)
    return pl.pallas_call(
        kernel,
        out_shape=(jax.ShapeDtypeStruct((512, 128), bf16), jax.ShapeDtypeStruct((512, 128), f32)),
        in_specs=[vmem, pl.BlockSpec(memory_space=pl.ANY), vmem],
        out_specs=(vmem, vmem),
        scratch_shapes=[pltpu.VMEM(s, t) for s, t in buffers] + [pltpu.SemaphoreType.DMA(s) for s in sems],
        compiler_params=pltpu.CompilerParams(
            collective_id=0, has_side_effects=True, vmem_limit_bytes=56 * 2**20
        ),
    )(activations, chunks, weight)


def solution(mesh):
    placed = (P(("dp", "col"), "row"), P(("dp", "row"), None, "col"), P("row", ("dp", "col")))
    return jax.shard_map(
        body,
        mesh=mesh,
        in_specs=placed,
        out_specs=(P("row", ("dp", "col")), P("row", ("dp", "col"))),
        check_vma=False,
    )
```

```python
import jax
import jax.numpy as jnp
from jax import lax
from jax.experimental import pallas as pl
from jax.experimental.pallas import tpu as pltpu
from jax.sharding import PartitionSpec as P

LOOKAHEAD = 4
PLACES = {"sym0": 5, "scatter0": 7, "gather0": 9, "product0": 11, "tile0": 14}


def nt(first, second):
    return lax.dot_general(first, second, (((1,), (1,)), ((), ())), preferred_element_type=jnp.float32)


def nn(first, second):
    return jnp.dot(first, second, preferred_element_type=jnp.float32)


def kernel(
    a_ref, c_ref, w_ref, g_out,
    a_all, a_t, c_all, own_part, part_send, part_recv,
    own, other, half, cs_send, cs_recv, zs_send, zs_recv, gram, own_prod, ps_send, ps_recv,
    local_sem, a_ss, a_rs, c_ss, c_rs, p_ss, p_rs,
    o_ss, o_rs, q_ss, q_rs, cs_ss, cs_rs, zs_ss, zs_rs, ag_ss, ag_rs, fw_ss, fw_rs, ps_ss, ps_rs,
):
    d, x, c = lax.axis_index("dp"), lax.axis_index("row"), lax.axis_index("col")
    y_lo, z, y_hi, core = d // 8, d % 8, c // 2, c % 2
    y = y_hi * 2 + y_lo

    def dev(x2, y2, z2, core2):
        return ((y2 % 2) * 8 + z2, x2, (y2 // 2) * 2 + core2)

    left, right = dev((x + 3) % 4, y, z, core), dev((x + 1) % 4, y, z, core)
    sibling = dev(x, y, z, 1 - core)
    hops_y = [dev(x, (y + k) % 4, z, core) for k in range(1, 4)]
    hops_z = [dev(x, y, (z + k) % 8, core) for k in range(1, 8)]

    barrier = pltpu.get_barrier_semaphore()
    for target in [left, right, sibling] + hops_y:
        pl.semaphore_signal(barrier, inc=1, device_id=target)

    @pl.loop(1, 16)
    def _(k):
        pl.semaphore_signal(barrier, inc=1, device_id=((d + k) % 16, x, c))

    @pl.when(x != y)
    def _():
        for k in range(4):
            pl.semaphore_signal(barrier, inc=1, device_id=dev(y, k, z, core))

    def remote(src, dst, ss, rs, target):
        return pltpu.make_async_remote_copy(
            src_ref=src, dst_ref=dst, send_sem=ss, recv_sem=rs, device_id=target
        )

    c_rows = pl.ds(pl.multiple_of(x * 512, 512), 512)
    copy_c = pltpu.make_async_copy(c_ref, c_all.at[:, c_rows, :], local_sem.at[0])
    copy_c.start()
    my_cols = pl.ds(pl.multiple_of(y * 128, 128), 128)
    own[0, :, my_cols] = w_ref[...]

    def put_transposed(block, ref):
        cols = pl.ds(pl.multiple_of(block * 512, 512), 512)
        a_t[:, cols] = ref[...].T

    put_transposed(c, a_ref)
    pl.semaphore_wait(barrier, 24)

    def col_of(k):
        return pl.ds(pl.multiple_of(k * 128, 128), 128)

    def chunk_rows(j):
        return pl.ds(j * 256, 256)

    def core_rows(j, h):
        return pl.ds(pl.multiple_of(j * 256 + h * 128, 128), 128)

    def own_copy(k, j, hop):
        view = own.at[k, chunk_rows(j), my_cols]
        return remote(
            view, view, o_ss.at[k, j, hop], o_rs.at[k, j, y], dev(x, (y + hop) % 4, z, core)
        )

    def other_copy(k, j, hop):
        return remote(
            own.at[k, chunk_rows(j), my_cols], other.at[k, chunk_rows(j), my_cols],
            q_ss.at[k, j, hop], q_rs.at[k, j, y], dev((x + hop) % 4, x, z, core),
        )

    def send_tile(k, j):
        for hop in (2, 1, 3):
            other_copy(k, j, hop).start()
            own_copy(k, j, hop).start()

    def wait_own(k, j):
        for hop in range(1, 4):
            source = (y + hop) % 4
            view = own.at[k, chunk_rows(j), col_of(source)]
            remote(view, view, o_ss.at[k, j, hop], o_rs.at[k, j, source], sibling).wait_recv()

    def wait_tile(k):
        for j in range(2):
            wait_own(k, j)

        @pl.when(x != y)
        def _():
            for j in range(2):
                for source in range(4):
                    view = other.at[k, chunk_rows(j), col_of(source)]
                    remote(view, view, q_ss.at[k, j, 0], q_rs.at[k, j, source], sibling).wait_recv()

        @pl.when(x == y)
        def _():
            other[k] = own[k]

    def swap_copy(k, j):
        return remote(cs_send.at[k, j], cs_recv.at[k, j], cs_ss.at[k, j], cs_rs.at[k, j], sibling)

    def sym(k, pairs):
        wait_tile(k)

        def block(rows):
            total = None
            for first, second in pairs:
                term = nt(own[first, rows, :], other[second])
                total = term if total is None else total + term
            return total

        for j in range(2):
            cs_send[k, j] = block(core_rows(j, 1 - core)).astype(jnp.bfloat16)
            swap_copy(k, j).start()
        for j in range(2):
            half[k, j] = block(core_rows(j, core))

    def scatter_copy(k, j, hop):
        target = (z + hop) % 8
        return remote(
            zs_send.at[k, j, target], zs_recv.at[k, j, z], zs_ss.at[k, j, hop], zs_rs.at[k, j, z],
            dev(x, y, target, core),
        )

    def scatter(k):
        for j in range(2):
            swap_copy(k, j).wait_recv()
            total = half[k, j] + cs_recv[k, j].astype(jnp.float32)
            half[k, j] = total
            zs_send[k, j] = total.astype(jnp.bfloat16).reshape(8, 16, 512)
            for hop in (4, 3, 5, 2, 6, 1, 7):
                scatter_copy(k, j, hop).start()

    def piece_rows(j, owner):
        return pl.ds(pl.multiple_of(j * 256 + core * 128 + owner * 16, 16), 16)

    def gather_copy(k, j, hop):
        view = gram.at[k, piece_rows(j, z), :]
        return remote(
            view, view, ag_ss.at[k, j, hop], ag_rs.at[k, j, z], dev(x, y, (z + hop) % 8, core)
        )

    def gather(k):
        for j in range(2):
            total = half[k, j, pl.ds(pl.multiple_of(z * 16, 16), 16), :]
            for hop in range(1, 8):
                source = (z + hop) % 8
                view = zs_recv.at[k, j, source]
                remote(view, view, zs_ss.at[k, j, hop], zs_rs.at[k, j, source], sibling).wait_recv()
                total = total + zs_recv[k, j, source].astype(jnp.float32)
            gram[k, piece_rows(j, z), :] = total.astype(jnp.bfloat16)
            for hop in (4, 3, 5, 2, 6, 1, 7):
                gather_copy(k, j, hop).start()

    def half_copy(k, j):
        view = gram.at[k, core_rows(j, core), :]
        return remote(view, view, fw_ss.at[k, j], fw_rs.at[k, j], sibling)

    def swap(k, j):
        for hop in range(1, 8):
            source = (z + hop) % 8
            view = gram.at[k, piece_rows(j, source), :]
            remote(view, view, ag_ss.at[k, j, hop], ag_rs.at[k, j, source], sibling).wait_recv()
        half_copy(k, j).start()

    def product_copy(k, j, hop):
        target = (y + hop) % 4
        return remote(
            ps_send.at[k, target, chunk_rows(j)], ps_recv.at[k, y, chunk_rows(j)],
            ps_ss.at[k, j, hop], ps_rs.at[k, j, y], dev(x, target, z, core),
        )

    def product(k, j, pairs):
        view = gram.at[k, core_rows(j, 1 - core), :]
        remote(view, view, fw_ss.at[k, j], fw_rs.at[k, j], sibling).wait_recv()
        rows = chunk_rows(j)
        for hop in (2, 1, 3, 0):
            target = (y + hop) % 4
            cols = col_of(target)
            total = None
            for matrix, panel in pairs:
                term = nn(gram[matrix, rows, :], other[panel, :, cols])
                total = term if total is None else total + term
            if hop:
                ps_send[k, target, rows] = total.astype(jnp.bfloat16)
                product_copy(k, j, hop).start()
            else:
                own_prod[k, rows, :] = total

    def swap_product(k, pairs):
        for j in range(2):
            swap(k, j)
            product(k, j, pairs)

    def result(k, j, tile):
        rows = chunk_rows(j)
        total = own_prod[k, rows, :]
        for hop in range(1, 4):
            source = (y + hop) % 4
            view = ps_recv.at[k, source, rows]
            remote(view, view, ps_ss.at[k, j, hop], ps_rs.at[k, j, source], sibling).wait_recv()
            total = total + ps_recv[k, source, rows].astype(jnp.float32)
        return 1.5 * own[tile, rows, my_cols].astype(jnp.float32) - 0.5 * total

    def finish_tile(k, tile, following):
        for j in range(2):
            own[following, chunk_rows(j), my_cols] = result(k, j, tile).astype(jnp.bfloat16)
            send_tile(following, j)

    def drain(k):
        for j in range(2):
            for hop in range(1, 4):
                own_copy(k, j, hop).wait_send()
                other_copy(k, j, hop).wait_send()
                product_copy(k, j, hop).wait_send()
            for hop in range(1, 8):
                scatter_copy(k, j, hop).wait_send()
                gather_copy(k, j, hop).wait_send()
            swap_copy(k, j).wait_send()
            half_copy(k, j).wait_send()

    far = dev(x, (y + 2) % 4, z, core)
    far_c = (c + 2) % 4
    a_far = remote(a_ref, a_all.at[c], a_ss.at[0], a_rs.at[c], far)
    a_sib = remote(a_ref, a_all.at[c], a_ss.at[1], a_rs.at[c], sibling)
    a_fwd = remote(a_all.at[far_c], a_all.at[far_c], a_ss.at[2], a_rs.at[far_c], sibling)
    sib_c = y_hi * 2 + 1 - core
    far_sib_c = (sib_c + 2) % 4

    def a_wait(block):
        view = a_all.at[block]
        remote(view, view, a_ss.at[0], a_rs.at[block], sibling).wait_recv()

    def chunk(i):
        return (d + 5 * (i + 1)) % 16

    def c_copy(i, way):
        view = c_all.at[chunk(i), c_rows, :]
        return remote(view, view, c_ss.at[i, way], c_rs.at[i, way], left if way else right)

    def rows_of(source):
        return pl.ds(pl.multiple_of(source * 512, 512), 512)

    def c_forward(i, way):
        source = (x + 3) % 4 if way == 0 else (x + 1) % 4
        view = c_all.at[chunk(i), rows_of(source), :]
        return remote(view, view, c_ss.at[i, 2], c_rs.at[i, 2], left if way else right)

    def c_wait(i, slot):
        view = c_all.at[chunk(i), rows_of(0), :]
        remote(view, view, c_ss.at[i, slot], c_rs.at[i, slot], sibling).wait_recv()

    def part_copy(i):
        a = chunk(i)
        return remote(part_send.at[a], part_recv.at[d], p_ss.at[a], p_rs.at[d], (a, x, c))

    send_tile(0, 0)
    send_tile(0, 1)
    a_far.start()
    a_sib.start()
    copy_c.wait()
    for i in range(LOOKAHEAD):
        c_copy(i, 0).start()
        c_copy(i, 1).start()
    a_wait(sib_c)
    put_transposed(sib_c, a_all.at[sib_c])

    stages = {
        "sym0": lambda: sym(0, [(0, 0)]),
        "scatter0": lambda: scatter(0),
        "gather0": lambda: gather(0),
        "product0": lambda: swap_product(0, [(0, 0)]),
        "tile0": lambda: finish_tile(0, 0, 1),
        "sym1": lambda: sym(1, [(1, 1)]),
    }

    @pl.loop(0, 17)
    def _(i):
        @pl.when(i + LOOKAHEAD < 16)
        def _():
            c_copy(i + LOOKAHEAD, 0).start()
            c_copy(i + LOOKAHEAD, 1).start()

        @pl.when(i < 16)
        def _():
            c_wait(i, 0)
            c_wait(i, 1)

            @pl.when(i % 2 == 0)
            def _():
                c_forward(i, 0).start()

            @pl.when(i % 2 == 1)
            def _():
                c_forward(i, 1).start()

        @pl.when(i == 0)
        def _():
            a_wait(far_c)
            a_fwd.start()
            put_transposed(far_c, a_all.at[far_c])
            a_wait(far_sib_c)
            put_transposed(far_sib_c, a_all.at[far_sib_c])

        @pl.when(i > 0)
        def _():
            c_wait(i - 1, 2)
            a = chunk(i - 1)
            block = nn(a_t[...], c_all[a])

            @pl.when(i < 16)
            def _():
                part_send[a] = block.astype(jnp.bfloat16)
                part_copy(i - 1).start()

            @pl.when(i == 16)
            def _():
                own_part[...] = block

        for name, place in PLACES.items():
            if place < 17:
                @pl.when(i == place)
                def _(name=name):
                    stages[name]()


    @pl.loop(1, 16)
    def _(k):
        source = (d + k) % 16
        view = part_recv.at[source]
        remote(view, view, p_ss.at[source], p_rs.at[source], sibling).wait_recv()

    for j in range(2):
        @pl.loop(j * 4, j * 4 + 4)
        def _(m):
            rows = pl.ds(pl.multiple_of(m * 64, 64), 64)
            total = own_part[rows, :]
            for k in range(1, 16):
                total = total + part_recv[(d + k) % 16, rows, :].astype(jnp.float32)
            own[2, rows, my_cols] = total.astype(jnp.bfloat16)

        send_tile(2, j)

    sym(1, [(1, 1)])
    scatter(1)
    for copy in (a_far, a_sib, a_fwd):
        copy.wait_send()

    @pl.loop(0, 16)
    def _(i):
        c_copy(i, 0).wait_send()
        c_copy(i, 1).wait_send()
        c_forward(i, 0).wait_send()

    @pl.loop(0, 15)
    def _(i):
        part_copy(i).wait_send()

    sym(2, [(2, 1), (1, 2)])
    gather(1)
    scatter(2)
    drain(0)
    swap(1, 0)
    swap(1, 1)
    gather(2)
    product(1, 0, [(1, 1)])
    product(1, 1, [(1, 1)])
    swap_product(2, [(1, 2), (2, 1)])
    finish_tile(2, 2, 3)
    for j in range(2):
        g_out[chunk_rows(j), pl.ds(128, 128)] = result(1, j, 1)
    drain(1)
    drain(2)
    sym(3, [(3, 0), (0, 3)])
    scatter(3)
    gather(3)
    swap_product(3, [(0, 3), (3, 0)])
    for j in range(2):
        g_out[chunk_rows(j), pl.ds(0, 128)] = result(3, j, 3)
    drain(3)


def body(activations, cotangent, weight):
    chunks = cotangent.transpose(1, 0, 2)
    bf16, f32 = jnp.bfloat16, jnp.float32
    sems = [
        (1,), (3,), (4,), (16, 3), (16, 3), (16,), (16,),
        (4, 2, 4), (4, 2, 4), (4, 2, 4), (4, 2, 4), (4, 2), (4, 2), (4, 2, 8), (4, 2, 8), (4, 2, 8), (4, 2, 8),
        (4, 2), (4, 2), (4, 2, 4), (4, 2, 4),
    ]
    buffers = [
        ((4, 512, 512), bf16), ((512, 2048), bf16), ((16, 2048, 128), bf16), ((512, 128), f32),
        ((16, 512, 128), bf16), ((16, 512, 128), bf16),
        ((4, 512, 512), bf16), ((4, 512, 512), bf16), ((4, 2, 128, 512), f32), ((4, 2, 128, 512), bf16),
        ((4, 2, 128, 512), bf16), ((4, 2, 8, 16, 512), bf16), ((4, 2, 8, 16, 512), bf16), ((4, 512, 512), bf16),
        ((4, 512, 128), f32), ((4, 4, 512, 128), bf16), ((4, 4, 512, 128), bf16),
    ]
    vmem = pl.BlockSpec(memory_space=pltpu.VMEM)
    both = pl.pallas_call(
        kernel,
        out_shape=jax.ShapeDtypeStruct((512, 256), f32),
        in_specs=[vmem, pl.BlockSpec(memory_space=pl.ANY), vmem],
        out_specs=vmem,
        scratch_shapes=[pltpu.VMEM(s, t) for s, t in buffers] + [pltpu.SemaphoreType.DMA(s) for s in sems],
        compiler_params=pltpu.CompilerParams(
            collective_id=0, has_side_effects=True, vmem_limit_bytes=56 * 2**20
        ),
    )(activations, chunks, weight)
    return both[:, 128:].astype(bf16), both[:, :128]


def solution(mesh):
    placed = (P(("dp", "col"), "row"), P(("dp", "row"), None, "col"), P("row", ("dp", "col")))
    return jax.shard_map(
        body,
        mesh=mesh,
        in_specs=placed,
        out_specs=(P("row", ("dp", "col")), P("row", ("dp", "col"))),
        check_vma=False,
    )
```

```python
import jax
import jax.numpy as jnp
from jax import lax
from jax.experimental import pallas as pl
from jax.experimental.pallas import tpu as pltpu
from jax.sharding import PartitionSpec as P

LOOKAHEAD = 4
LAG = 4
PLACES = {"sym0": 6, "scatter0": 8, "gather0": 10, "product0": 12, "tile0": 15}


def nt(first, second):
    return lax.dot_general(first, second, (((1,), (1,)), ((), ())), preferred_element_type=jnp.float32)


def nn(first, second):
    return jnp.dot(first, second, preferred_element_type=jnp.float32)


def kernel(
    a_ref, c_ref, w_ref, g_out,
    a_all, a_t, c_all, own_part, part_sum, part_send, part_recv,
    own, other, half, cs_send, cs_recv, zs_send, zs_recv, gram, own_prod, ps_send, ps_recv,
    local_sem, a_ss, a_rs, c_ss, c_rs, p_ss, p_rs,
    o_ss, o_rs, q_ss, q_rs, cs_ss, cs_rs, zs_ss, zs_rs, ag_ss, ag_rs, fw_ss, fw_rs, ps_ss, ps_rs,
):
    d, x, c = lax.axis_index("dp"), lax.axis_index("row"), lax.axis_index("col")
    y_lo, z, y_hi, core = d // 8, d % 8, c // 2, c % 2
    y = y_hi * 2 + y_lo

    def dev(x2, y2, z2, core2):
        return ((y2 % 2) * 8 + z2, x2, (y2 // 2) * 2 + core2)

    left, right = dev((x + 3) % 4, y, z, core), dev((x + 1) % 4, y, z, core)
    sibling = dev(x, y, z, 1 - core)
    hops_y = [dev(x, (y + k) % 4, z, core) for k in range(1, 4)]
    hops_z = [dev(x, y, (z + k) % 8, core) for k in range(1, 8)]

    barrier = pltpu.get_barrier_semaphore()
    for target in [left, right, sibling] + hops_y:
        pl.semaphore_signal(barrier, inc=1, device_id=target)

    @pl.loop(1, 16)
    def _(k):
        pl.semaphore_signal(barrier, inc=1, device_id=((d + k) % 16, x, c))

    @pl.when(x != y)
    def _():
        for k in range(4):
            pl.semaphore_signal(barrier, inc=1, device_id=dev(y, k, z, core))

    def remote(src, dst, ss, rs, target):
        return pltpu.make_async_remote_copy(
            src_ref=src, dst_ref=dst, send_sem=ss, recv_sem=rs, device_id=target
        )

    c_rows = pl.ds(pl.multiple_of(x * 512, 512), 512)
    copy_c = pltpu.make_async_copy(c_ref, c_all.at[:, c_rows, :], local_sem.at[0])
    copy_c.start()
    my_cols = pl.ds(pl.multiple_of(y * 128, 128), 128)
    own[0, :, my_cols] = w_ref[...]

    def put_transposed(block, ref):
        cols = pl.ds(pl.multiple_of(block * 512, 512), 512)
        a_t[:, cols] = ref[...].T

    put_transposed(c, a_ref)
    pl.semaphore_wait(barrier, 24)

    def col_of(k):
        return pl.ds(pl.multiple_of(k * 128, 128), 128)

    def chunk_rows(j):
        return pl.ds(j * 256, 256)

    def core_rows(j, h):
        return pl.ds(pl.multiple_of(j * 256 + h * 128, 128), 128)

    def own_copy(k, j, hop):
        view = own.at[k, chunk_rows(j), my_cols]
        return remote(
            view, view, o_ss.at[k, j, hop], o_rs.at[k, j, y], dev(x, (y + hop) % 4, z, core)
        )

    def other_copy(k, j, hop):
        return remote(
            own.at[k, chunk_rows(j), my_cols], other.at[k, chunk_rows(j), my_cols],
            q_ss.at[k, j, hop], q_rs.at[k, j, y], dev((x + hop) % 4, x, z, core),
        )

    def send_tile(k, j):
        for hop in (2, 1, 3):
            other_copy(k, j, hop).start()
            own_copy(k, j, hop).start()

    def wait_own(k, j):
        for hop in range(1, 4):
            source = (y + hop) % 4
            view = own.at[k, chunk_rows(j), col_of(source)]
            remote(view, view, o_ss.at[k, j, hop], o_rs.at[k, j, source], sibling).wait_recv()

    def wait_tile(k):
        for j in range(2):
            wait_own(k, j)

        @pl.when(x != y)
        def _():
            for j in range(2):
                for source in range(4):
                    view = other.at[k, chunk_rows(j), col_of(source)]
                    remote(view, view, q_ss.at[k, j, 0], q_rs.at[k, j, source], sibling).wait_recv()

        @pl.when(x == y)
        def _():
            other[k] = own[k]

    def swap_copy(k, j):
        return remote(cs_send.at[k, j], cs_recv.at[k, j], cs_ss.at[k, j], cs_rs.at[k, j], sibling)

    def sym(k, pairs):
        wait_tile(k)

        def block(rows):
            total = None
            for first, second in pairs:
                term = nt(own[first, rows, :], other[second])
                total = term if total is None else total + term
            return total

        for j in range(2):
            cs_send[k, j] = block(core_rows(j, 1 - core)).astype(jnp.bfloat16)
            swap_copy(k, j).start()
        for j in range(2):
            half[k, j] = block(core_rows(j, core))

    def scatter_copy(k, j, hop):
        target = (z + hop) % 8
        return remote(
            zs_send.at[k, j, target], zs_recv.at[k, j, z], zs_ss.at[k, j, hop], zs_rs.at[k, j, z],
            dev(x, y, target, core),
        )

    def scatter(k):
        for j in range(2):
            swap_copy(k, j).wait_recv()
            total = half[k, j] + cs_recv[k, j].astype(jnp.float32)
            half[k, j] = total
            zs_send[k, j] = total.astype(jnp.bfloat16).reshape(8, 16, 512)
            for hop in (4, 3, 5, 2, 6, 1, 7):
                scatter_copy(k, j, hop).start()

    def piece_rows(j, owner):
        return pl.ds(pl.multiple_of(j * 256 + core * 128 + owner * 16, 16), 16)

    def gather_copy(k, j, hop):
        view = gram.at[k, piece_rows(j, z), :]
        return remote(
            view, view, ag_ss.at[k, j, hop], ag_rs.at[k, j, z], dev(x, y, (z + hop) % 8, core)
        )

    def gather(k):
        for j in range(2):
            total = half[k, j, pl.ds(pl.multiple_of(z * 16, 16), 16), :]
            for hop in range(1, 8):
                source = (z + hop) % 8
                view = zs_recv.at[k, j, source]
                remote(view, view, zs_ss.at[k, j, hop], zs_rs.at[k, j, source], sibling).wait_recv()
                total = total + zs_recv[k, j, source].astype(jnp.float32)
            gram[k, piece_rows(j, z), :] = total.astype(jnp.bfloat16)
            for hop in (4, 3, 5, 2, 6, 1, 7):
                gather_copy(k, j, hop).start()

    def half_copy(k, j):
        view = gram.at[k, core_rows(j, core), :]
        return remote(view, view, fw_ss.at[k, j], fw_rs.at[k, j], sibling)

    def swap(k, j):
        for hop in range(1, 8):
            source = (z + hop) % 8
            view = gram.at[k, piece_rows(j, source), :]
            remote(view, view, ag_ss.at[k, j, hop], ag_rs.at[k, j, source], sibling).wait_recv()
        half_copy(k, j).start()

    def product_copy(k, j, hop):
        target = (y + hop) % 4
        return remote(
            ps_send.at[k, target, chunk_rows(j)], ps_recv.at[k, y, chunk_rows(j)],
            ps_ss.at[k, j, hop], ps_rs.at[k, j, y], dev(x, target, z, core),
        )

    def product(k, j, pairs):
        view = gram.at[k, core_rows(j, 1 - core), :]
        remote(view, view, fw_ss.at[k, j], fw_rs.at[k, j], sibling).wait_recv()
        rows = chunk_rows(j)
        for hop in (2, 1, 3, 0):
            target = (y + hop) % 4
            cols = col_of(target)
            total = None
            for matrix, panel in pairs:
                term = nn(gram[matrix, rows, :], other[panel, :, cols])
                total = term if total is None else total + term
            if hop:
                ps_send[k, target, rows] = total.astype(jnp.bfloat16)
                product_copy(k, j, hop).start()
            else:
                own_prod[k, rows, :] = total

    def swap_product(k, pairs):
        for j in range(2):
            swap(k, j)
            product(k, j, pairs)

    def result(k, j, tile):
        rows = chunk_rows(j)
        total = own_prod[k, rows, :]
        for hop in range(1, 4):
            source = (y + hop) % 4
            view = ps_recv.at[k, source, rows]
            remote(view, view, ps_ss.at[k, j, hop], ps_rs.at[k, j, source], sibling).wait_recv()
            total = total + ps_recv[k, source, rows].astype(jnp.float32)
        return 1.5 * own[tile, rows, my_cols].astype(jnp.float32) - 0.5 * total

    def finish_tile(k, tile, following):
        for j in range(2):
            own[following, chunk_rows(j), my_cols] = result(k, j, tile).astype(jnp.bfloat16)
            send_tile(following, j)

    def drain(k):
        for j in range(2):
            for hop in range(1, 4):
                own_copy(k, j, hop).wait_send()
                other_copy(k, j, hop).wait_send()
                product_copy(k, j, hop).wait_send()
            for hop in range(1, 8):
                scatter_copy(k, j, hop).wait_send()
                gather_copy(k, j, hop).wait_send()
            swap_copy(k, j).wait_send()
            half_copy(k, j).wait_send()

    far = dev(x, (y + 2) % 4, z, core)
    far_c = (c + 2) % 4
    a_far = remote(a_ref, a_all.at[c], a_ss.at[0], a_rs.at[c], far)
    a_sib = remote(a_ref, a_all.at[c], a_ss.at[1], a_rs.at[c], sibling)
    a_fwd = remote(a_all.at[far_c], a_all.at[far_c], a_ss.at[2], a_rs.at[far_c], sibling)
    sib_c = y_hi * 2 + 1 - core
    far_sib_c = (sib_c + 2) % 4

    def a_wait(block):
        view = a_all.at[block]
        remote(view, view, a_ss.at[0], a_rs.at[block], sibling).wait_recv()

    def chunk(i):
        return (d + 5 * (i + 1)) % 16

    def c_copy(i, way):
        view = c_all.at[chunk(i), c_rows, :]
        return remote(view, view, c_ss.at[i, way], c_rs.at[i, way], left if way else right)

    def rows_of(source):
        return pl.ds(pl.multiple_of(source * 512, 512), 512)

    def c_forward(i, way):
        source = (x + 3) % 4 if way == 0 else (x + 1) % 4
        view = c_all.at[chunk(i), rows_of(source), :]
        return remote(view, view, c_ss.at[i, 2], c_rs.at[i, 2], left if way else right)

    def c_wait(i, slot):
        view = c_all.at[chunk(i), rows_of(0), :]
        remote(view, view, c_ss.at[i, slot], c_rs.at[i, slot], sibling).wait_recv()

    def part_copy(i):
        a = chunk(i)
        return remote(part_send.at[a], part_recv.at[d], p_ss.at[a], p_rs.at[d], (a, x, c))

    copy_c.wait()
    c_copy(0, 0).start()
    c_copy(0, 1).start()
    send_tile(0, 0)
    send_tile(0, 1)
    a_far.start()
    a_sib.start()
    for i in range(1, LOOKAHEAD):
        c_copy(i, 0).start()
        c_copy(i, 1).start()
    a_wait(sib_c)
    put_transposed(sib_c, a_all.at[sib_c])

    stages = {
        "sym0": lambda: sym(0, [(0, 0)]),
        "scatter0": lambda: scatter(0),
        "gather0": lambda: gather(0),
        "product0": lambda: swap_product(0, [(0, 0)]),
        "tile0": lambda: finish_tile(0, 0, 1),
        "sym1": lambda: sym(1, [(1, 1)]),
    }

    def source_of(k):
        return (d + 80 - 5 * (k + 1)) % 16

    def part_wait(k):
        source = source_of(k)
        view = part_recv.at[source]
        remote(view, view, p_ss.at[source], p_rs.at[source], sibling).wait_recv()

    part_sum[...] = jnp.zeros_like(part_sum)

    @pl.loop(0, 17)
    def _(i):
        @pl.when(i + LOOKAHEAD < 16)
        def _():
            c_copy(i + LOOKAHEAD, 0).start()
            c_copy(i + LOOKAHEAD, 1).start()

        @pl.when(i < 16)
        def _():
            c_wait(i, 0)
            c_wait(i, 1)

            @pl.when(i % 2 == 0)
            def _():
                c_forward(i, 0).start()

            @pl.when(i % 2 == 1)
            def _():
                c_forward(i, 1).start()

        @pl.when(i == 0)
        def _():
            a_wait(far_c)
            a_fwd.start()
            put_transposed(far_c, a_all.at[far_c])
            a_wait(far_sib_c)
            put_transposed(far_sib_c, a_all.at[far_sib_c])

        @pl.when(i > 0)
        def _():
            c_wait(i - 1, 2)
            a = chunk(i - 1)
            block = nn(a_t[...], c_all[a])

            @pl.when(i < 16)
            def _():
                part_send[a] = block.astype(jnp.bfloat16)
                part_copy(i - 1).start()

            @pl.when(i == 16)
            def _():
                own_part[...] = block

        @pl.when(i > LAG)
        def _():
            part_wait(i - LAG - 1)
            part_sum[...] += part_recv[source_of(i - LAG - 1)].astype(jnp.float32)

        for name, place in PLACES.items():
            if place < 17:
                @pl.when(i == place)
                def _(name=name):
                    stages[name]()


    for k in range(16 - LAG, 15):
        part_wait(k)

    for j in range(2):
        @pl.loop(j * 4, j * 4 + 4)
        def _(m):
            rows = pl.ds(pl.multiple_of(m * 64, 64), 64)
            total = own_part[rows, :] + part_sum[rows, :]
            for k in range(16 - LAG, 15):
                total = total + part_recv[source_of(k), rows, :].astype(jnp.float32)
            own[2, rows, my_cols] = total.astype(jnp.bfloat16)

        send_tile(2, j)

    sym(1, [(1, 1)])
    scatter(1)
    for copy in (a_far, a_sib, a_fwd):
        copy.wait_send()

    @pl.loop(0, 16)
    def _(i):
        c_copy(i, 0).wait_send()
        c_copy(i, 1).wait_send()
        c_forward(i, 0).wait_send()

    @pl.loop(0, 15)
    def _(i):
        part_copy(i).wait_send()

    sym(2, [(2, 1), (1, 2)])
    gather(1)
    scatter(2)
    drain(0)
    swap(1, 0)
    swap(1, 1)
    gather(2)
    product(1, 0, [(1, 1)])
    product(1, 1, [(1, 1)])
    swap_product(2, [(1, 2), (2, 1)])
    finish_tile(2, 2, 3)
    for j in range(2):
        g_out[chunk_rows(j), pl.ds(128, 128)] = result(1, j, 1)
    drain(1)
    drain(2)
    sym(3, [(3, 0), (0, 3)])
    scatter(3)
    gather(3)
    swap_product(3, [(0, 3), (3, 0)])
    for j in range(2):
        g_out[chunk_rows(j), pl.ds(0, 128)] = result(3, j, 3)
    drain(3)


def body(activations, cotangent, weight):
    chunks = cotangent.transpose(1, 0, 2)
    bf16, f32 = jnp.bfloat16, jnp.float32
    sems = [
        (1,), (3,), (4,), (16, 3), (16, 3), (16,), (16,),
        (4, 2, 4), (4, 2, 4), (4, 2, 4), (4, 2, 4), (4, 2), (4, 2), (4, 2, 8), (4, 2, 8), (4, 2, 8), (4, 2, 8),
        (4, 2), (4, 2), (4, 2, 4), (4, 2, 4),
    ]
    buffers = [
        ((4, 512, 512), bf16), ((512, 2048), bf16), ((16, 2048, 128), bf16), ((512, 128), f32), ((512, 128), f32),
        ((16, 512, 128), bf16), ((16, 512, 128), bf16),
        ((4, 512, 512), bf16), ((4, 512, 512), bf16), ((4, 2, 128, 512), f32), ((4, 2, 128, 512), bf16),
        ((4, 2, 128, 512), bf16), ((4, 2, 8, 16, 512), bf16), ((4, 2, 8, 16, 512), bf16), ((4, 512, 512), bf16),
        ((4, 512, 128), f32), ((4, 4, 512, 128), bf16), ((4, 4, 512, 128), bf16),
    ]
    vmem = pl.BlockSpec(memory_space=pltpu.VMEM)
    both = pl.pallas_call(
        kernel,
        out_shape=jax.ShapeDtypeStruct((512, 256), f32),
        in_specs=[vmem, pl.BlockSpec(memory_space=pl.ANY), vmem],
        out_specs=vmem,
        scratch_shapes=[pltpu.VMEM(s, t) for s, t in buffers] + [pltpu.SemaphoreType.DMA(s) for s in sems],
        compiler_params=pltpu.CompilerParams(
            collective_id=0, has_side_effects=True, vmem_limit_bytes=56 * 2**20
        ),
    )(activations, chunks, weight)
    return both[:, 128:].astype(bf16), both[:, :128]


def solution(mesh):
    placed = (P(("dp", "col"), "row"), P(("dp", "row"), None, "col"), P("row", ("dp", "col")))
    return jax.shard_map(
        body,
        mesh=mesh,
        in_specs=placed,
        out_specs=(P("row", ("dp", "col")), P("row", ("dp", "col"))),
        check_vma=False,
    )
```

```python
import jax
import jax.numpy as jnp
from jax import lax
from jax.experimental import pallas as pl
from jax.experimental.pallas import tpu as pltpu
from jax.sharding import PartitionSpec as P

LOOKAHEAD = 4
PLACES = {"sym0": 5, "scatter0": 7, "gather0": 9, "product0": 11, "tile0": 14}


def nt(first, second):
    return lax.dot_general(first, second, (((1,), (1,)), ((), ())), preferred_element_type=jnp.float32)


def nn(first, second):
    return jnp.dot(first, second, preferred_element_type=jnp.float32)


def kernel(
    a_ref, c_ref, w_ref, g_out,
    a_all, a_t, c_all, own_part, part_send, part_recv,
    own, other, half, cs_send, cs_recv, zs_send, zs_recv, gram, prior, own_prod, ps_send, ps_recv,
    local_sem, a_ss, a_rs, c_ss, c_rs, p_ss, p_rs,
    o_ss, o_rs, q_ss, q_rs, cs_ss, cs_rs, zs_ss, zs_rs, ag_ss, ag_rs, fw_ss, fw_rs, ps_ss, ps_rs,
):
    d, x, c = lax.axis_index("dp"), lax.axis_index("row"), lax.axis_index("col")
    y_lo, z, y_hi, core = d // 8, d % 8, c // 2, c % 2
    y = y_hi * 2 + y_lo

    def dev(x2, y2, z2, core2):
        return ((y2 % 2) * 8 + z2, x2, (y2 // 2) * 2 + core2)

    left, right = dev((x + 3) % 4, y, z, core), dev((x + 1) % 4, y, z, core)
    sibling = dev(x, y, z, 1 - core)
    hops_y = [dev(x, (y + k) % 4, z, core) for k in range(1, 4)]
    hops_z = [dev(x, y, (z + k) % 8, core) for k in range(1, 8)]

    barrier = pltpu.get_barrier_semaphore()
    for target in [left, right, sibling] + hops_y:
        pl.semaphore_signal(barrier, inc=1, device_id=target)

    @pl.loop(1, 16)
    def _(k):
        pl.semaphore_signal(barrier, inc=1, device_id=((d + k) % 16, x, c))

    @pl.when(x != y)
    def _():
        for k in range(4):
            pl.semaphore_signal(barrier, inc=1, device_id=dev(y, k, z, core))

    def remote(src, dst, ss, rs, target):
        return pltpu.make_async_remote_copy(
            src_ref=src, dst_ref=dst, send_sem=ss, recv_sem=rs, device_id=target
        )

    c_rows = pl.ds(pl.multiple_of(x * 512, 512), 512)
    copy_c = pltpu.make_async_copy(c_ref, c_all.at[:, c_rows, :], local_sem.at[0])
    copy_c.start()
    my_cols = pl.ds(pl.multiple_of(y * 128, 128), 128)
    own[0, :, my_cols] = w_ref[...]

    def put_transposed(block, ref):
        cols = pl.ds(pl.multiple_of(block * 512, 512), 512)
        a_t[:, cols] = ref[...].T

    put_transposed(c, a_ref)
    pl.semaphore_wait(barrier, 24)

    def col_of(k):
        return pl.ds(pl.multiple_of(k * 128, 128), 128)

    def chunk_rows(j):
        return pl.ds(j * 256, 256)

    def core_rows(j, h):
        return pl.ds(pl.multiple_of(j * 256 + h * 128, 128), 128)

    def own_copy(k, j, hop):
        view = own.at[k, chunk_rows(j), my_cols]
        return remote(
            view, view, o_ss.at[k, j, hop], o_rs.at[k, j, y], dev(x, (y + hop) % 4, z, core)
        )

    def other_copy(k, j, hop):
        return remote(
            own.at[k, chunk_rows(j), my_cols], other.at[k, chunk_rows(j), my_cols],
            q_ss.at[k, j, hop], q_rs.at[k, j, y], dev((x + hop) % 4, x, z, core),
        )

    def send_tile(k, j):
        for hop in (2, 1, 3):
            other_copy(k, j, hop).start()
            own_copy(k, j, hop).start()

    def wait_own(k, j):
        for hop in range(1, 4):
            source = (y + hop) % 4
            view = own.at[k, chunk_rows(j), col_of(source)]
            remote(view, view, o_ss.at[k, j, hop], o_rs.at[k, j, source], sibling).wait_recv()

    def wait_tile(k):
        for j in range(2):
            wait_own(k, j)

        @pl.when(x != y)
        def _():
            for j in range(2):
                for source in range(4):
                    view = other.at[k, chunk_rows(j), col_of(source)]
                    remote(view, view, q_ss.at[k, j, 0], q_rs.at[k, j, source], sibling).wait_recv()

        @pl.when(x == y)
        def _():
            other[k] = own[k]

    def swap_copy(k, j):
        return remote(cs_send.at[k, j], cs_recv.at[k, j], cs_ss.at[k, j], cs_rs.at[k, j], sibling)

    def sym(k, pairs):
        wait_tile(k)

        def block(rows):
            total = None
            for first, second in pairs:
                term = nt(own[first, rows, :], other[second])
                total = term if total is None else total + term
            return total

        for j in range(2):
            cs_send[k, j] = block(core_rows(j, 1 - core)).astype(jnp.bfloat16)
            swap_copy(k, j).start()
        for j in range(2):
            half[k, j] = block(core_rows(j, core))

    def scatter_copy(k, j, hop):
        target = (z + hop) % 8
        return remote(
            zs_send.at[k, j, target], zs_recv.at[k, j, z], zs_ss.at[k, j, hop], zs_rs.at[k, j, z],
            dev(x, y, target, core),
        )

    def scatter(k):
        for j in range(2):
            swap_copy(k, j).wait_recv()
            total = half[k, j] + cs_recv[k, j].astype(jnp.float32)
            half[k, j] = total
            zs_send[k, j] = total.astype(jnp.bfloat16).reshape(8, 16, 512)
            for hop in (4, 3, 5, 2, 6, 1, 7):
                scatter_copy(k, j, hop).start()

    def piece_rows(j, owner):
        return pl.ds(pl.multiple_of(j * 256 + core * 128 + owner * 16, 16), 16)

    def gather_copy(k, j, hop):
        view = gram.at[k, piece_rows(j, z), :]
        return remote(
            view, view, ag_ss.at[k, j, hop], ag_rs.at[k, j, z], dev(x, y, (z + hop) % 8, core)
        )

    def gather(k):
        for j in range(2):
            total = half[k, j, pl.ds(pl.multiple_of(z * 16, 16), 16), :]
            for hop in range(1, 8):
                source = (z + hop) % 8
                view = zs_recv.at[k, j, source]
                remote(view, view, zs_ss.at[k, j, hop], zs_rs.at[k, j, source], sibling).wait_recv()
                total = total + zs_recv[k, j, source].astype(jnp.float32)
            gram[k, piece_rows(j, z), :] = total.astype(jnp.bfloat16)
            for hop in (4, 3, 5, 2, 6, 1, 7):
                gather_copy(k, j, hop).start()

    def half_copy(k, j):
        view = gram.at[k, core_rows(j, core), :]
        return remote(view, view, fw_ss.at[k, j], fw_rs.at[k, j], sibling)

    def swap(k, j):
        for hop in range(1, 8):
            source = (z + hop) % 8
            view = gram.at[k, piece_rows(j, source), :]
            remote(view, view, ag_ss.at[k, j, hop], ag_rs.at[k, j, source], sibling).wait_recv()
        half_copy(k, j).start()

    def product_copy(k, j, hop):
        target = (y + hop) % 4
        return remote(
            ps_send.at[k, target, chunk_rows(j)], ps_recv.at[k, y, chunk_rows(j)],
            ps_ss.at[k, j, hop], ps_rs.at[k, j, y], dev(x, target, z, core),
        )

    def product(k, j, pairs):
        view = gram.at[k, core_rows(j, 1 - core), :]
        remote(view, view, fw_ss.at[k, j], fw_rs.at[k, j], sibling).wait_recv()
        rows = chunk_rows(j)
        for hop in (2, 1, 3, 0):
            target = (y + hop) % 4
            cols = col_of(target)
            total = prior[rows, cols] if k >= 2 else None
            for matrix, panel in pairs:
                term = nn(gram[matrix, rows, :], other[panel, :, cols])
                total = term if total is None else total + term
            if hop:
                ps_send[k, target, rows] = total.astype(jnp.bfloat16)
                product_copy(k, j, hop).start()
            else:
                own_prod[k, rows, :] = total

    def prepare(matrix, panel):
        for j in range(2):
            prior[chunk_rows(j), :] = nn(gram[matrix, chunk_rows(j), :], other[panel])

    def swap_product(k, pairs):
        for j in range(2):
            swap(k, j)
            product(k, j, pairs)

    def result(k, j, tile):
        rows = chunk_rows(j)
        total = own_prod[k, rows, :]
        for hop in range(1, 4):
            source = (y + hop) % 4
            view = ps_recv.at[k, source, rows]
            remote(view, view, ps_ss.at[k, j, hop], ps_rs.at[k, j, source], sibling).wait_recv()
            total = total + ps_recv[k, source, rows].astype(jnp.float32)
        return 1.5 * own[tile, rows, my_cols].astype(jnp.float32) - 0.5 * total

    def finish_tile(k, tile, following):
        for j in range(2):
            own[following, chunk_rows(j), my_cols] = result(k, j, tile).astype(jnp.bfloat16)
            send_tile(following, j)

    def drain(k):
        for j in range(2):
            for hop in range(1, 4):
                own_copy(k, j, hop).wait_send()
                other_copy(k, j, hop).wait_send()
                product_copy(k, j, hop).wait_send()
            for hop in range(1, 8):
                scatter_copy(k, j, hop).wait_send()
                gather_copy(k, j, hop).wait_send()
            swap_copy(k, j).wait_send()
            half_copy(k, j).wait_send()

    far = dev(x, (y + 2) % 4, z, core)
    far_c = (c + 2) % 4
    a_far = remote(a_ref, a_all.at[c], a_ss.at[0], a_rs.at[c], far)
    a_sib = remote(a_ref, a_all.at[c], a_ss.at[1], a_rs.at[c], sibling)
    a_fwd = remote(a_all.at[far_c], a_all.at[far_c], a_ss.at[2], a_rs.at[far_c], sibling)
    sib_c = y_hi * 2 + 1 - core
    far_sib_c = (sib_c + 2) % 4

    def a_wait(block):
        view = a_all.at[block]
        remote(view, view, a_ss.at[0], a_rs.at[block], sibling).wait_recv()

    def chunk(i):
        return (d + 5 * (i + 1)) % 16

    def c_copy(i, way):
        view = c_all.at[chunk(i), c_rows, :]
        return remote(view, view, c_ss.at[i, way], c_rs.at[i, way], left if way else right)

    def rows_of(source):
        return pl.ds(pl.multiple_of(source * 512, 512), 512)

    def c_forward(i, way):
        source = (x + 3) % 4 if way == 0 else (x + 1) % 4
        view = c_all.at[chunk(i), rows_of(source), :]
        return remote(view, view, c_ss.at[i, 2], c_rs.at[i, 2], left if way else right)

    def c_wait(i, slot):
        view = c_all.at[chunk(i), rows_of(0), :]
        remote(view, view, c_ss.at[i, slot], c_rs.at[i, slot], sibling).wait_recv()

    def part_copy(i):
        a = chunk(i)
        return remote(part_send.at[a], part_recv.at[d], p_ss.at[a], p_rs.at[d], (a, x, c))

    send_tile(0, 0)
    send_tile(0, 1)
    a_far.start()
    a_sib.start()
    copy_c.wait()
    for i in range(LOOKAHEAD):
        c_copy(i, 0).start()
        c_copy(i, 1).start()
    a_wait(sib_c)
    put_transposed(sib_c, a_all.at[sib_c])

    stages = {
        "sym0": lambda: sym(0, [(0, 0)]),
        "scatter0": lambda: scatter(0),
        "gather0": lambda: gather(0),
        "product0": lambda: swap_product(0, [(0, 0)]),
        "tile0": lambda: finish_tile(0, 0, 1),
        "sym1": lambda: sym(1, [(1, 1)]),
    }

    @pl.loop(0, 17)
    def _(i):
        @pl.when(i + LOOKAHEAD < 16)
        def _():
            c_copy(i + LOOKAHEAD, 0).start()
            c_copy(i + LOOKAHEAD, 1).start()

        @pl.when(i < 16)
        def _():
            c_wait(i, 0)
            c_wait(i, 1)

            @pl.when(i % 2 == 0)
            def _():
                c_forward(i, 0).start()

            @pl.when(i % 2 == 1)
            def _():
                c_forward(i, 1).start()

        @pl.when(i == 0)
        def _():
            a_wait(far_c)
            a_fwd.start()
            put_transposed(far_c, a_all.at[far_c])
            a_wait(far_sib_c)
            put_transposed(far_sib_c, a_all.at[far_sib_c])

        @pl.when(i > 0)
        def _():
            c_wait(i - 1, 2)
            a = chunk(i - 1)
            block = nn(a_t[...], c_all[a])

            @pl.when(i < 16)
            def _():
                part_send[a] = block.astype(jnp.bfloat16)
                part_copy(i - 1).start()

            @pl.when(i == 16)
            def _():
                own_part[...] = block

        for name, place in PLACES.items():
            if place < 17:
                @pl.when(i == place)
                def _(name=name):
                    stages[name]()


    @pl.loop(1, 16)
    def _(k):
        source = (d + k) % 16
        view = part_recv.at[source]
        remote(view, view, p_ss.at[source], p_rs.at[source], sibling).wait_recv()

    for j in range(2):
        @pl.loop(j * 4, j * 4 + 4)
        def _(m):
            rows = pl.ds(pl.multiple_of(m * 64, 64), 64)
            total = own_part[rows, :]
            for k in range(1, 16):
                total = total + part_recv[(d + k) % 16, rows, :].astype(jnp.float32)
            own[2, rows, my_cols] = total.astype(jnp.bfloat16)

        send_tile(2, j)

    sym(1, [(1, 1)])
    scatter(1)
    for copy in (a_far, a_sib, a_fwd):
        copy.wait_send()

    @pl.loop(0, 16)
    def _(i):
        c_copy(i, 0).wait_send()
        c_copy(i, 1).wait_send()
        c_forward(i, 0).wait_send()

    @pl.loop(0, 15)
    def _(i):
        part_copy(i).wait_send()

    sym(2, [(2, 1), (1, 2)])
    gather(1)
    scatter(2)
    drain(0)
    swap(1, 0)
    swap(1, 1)
    gather(2)
    product(1, 0, [(1, 1)])
    product(1, 1, [(1, 1)])
    prepare(1, 2)
    swap_product(2, [(2, 1)])
    finish_tile(2, 2, 3)
    for j in range(2):
        g_out[chunk_rows(j), pl.ds(128, 128)] = result(1, j, 1)
    drain(1)
    drain(2)
    sym(3, [(3, 0), (0, 3)])
    scatter(3)
    gather(3)
    prepare(0, 3)
    swap_product(3, [(3, 0)])
    for j in range(2):
        g_out[chunk_rows(j), pl.ds(0, 128)] = result(3, j, 3)
    drain(3)


def body(activations, cotangent, weight):
    chunks = cotangent.transpose(1, 0, 2)
    bf16, f32 = jnp.bfloat16, jnp.float32
    sems = [
        (1,), (3,), (4,), (16, 3), (16, 3), (16,), (16,),
        (4, 2, 4), (4, 2, 4), (4, 2, 4), (4, 2, 4), (4, 2), (4, 2), (4, 2, 8), (4, 2, 8), (4, 2, 8), (4, 2, 8),
        (4, 2), (4, 2), (4, 2, 4), (4, 2, 4),
    ]
    buffers = [
        ((4, 512, 512), bf16), ((512, 2048), bf16), ((16, 2048, 128), bf16), ((512, 128), f32),
        ((16, 512, 128), bf16), ((16, 512, 128), bf16),
        ((4, 512, 512), bf16), ((4, 512, 512), bf16), ((4, 2, 128, 512), f32), ((4, 2, 128, 512), bf16),
        ((4, 2, 128, 512), bf16), ((4, 2, 8, 16, 512), bf16), ((4, 2, 8, 16, 512), bf16), ((4, 512, 512), bf16),
        ((512, 512), f32), ((4, 512, 128), f32), ((4, 4, 512, 128), bf16), ((4, 4, 512, 128), bf16),
    ]
    vmem = pl.BlockSpec(memory_space=pltpu.VMEM)
    both = pl.pallas_call(
        kernel,
        out_shape=jax.ShapeDtypeStruct((512, 256), f32),
        in_specs=[vmem, pl.BlockSpec(memory_space=pl.ANY), vmem],
        out_specs=vmem,
        scratch_shapes=[pltpu.VMEM(s, t) for s, t in buffers] + [pltpu.SemaphoreType.DMA(s) for s in sems],
        compiler_params=pltpu.CompilerParams(
            collective_id=0, has_side_effects=True, vmem_limit_bytes=56 * 2**20
        ),
    )(activations, chunks, weight)
    return both[:, 128:].astype(bf16), both[:, :128]


def solution(mesh):
    placed = (P(("dp", "col"), "row"), P(("dp", "row"), None, "col"), P("row", ("dp", "col")))
    return jax.shard_map(
        body,
        mesh=mesh,
        in_specs=placed,
        out_specs=(P("row", ("dp", "col")), P("row", ("dp", "col"))),
        check_vma=False,
    )
```

```python
import jax
import jax.numpy as jnp
from jax import lax
from jax.experimental import pallas as pl
from jax.experimental.pallas import tpu as pltpu
from jax.sharding import PartitionSpec as P

LOOKAHEAD = 4
LAG = 4
PLACES = {"sym0": 6, "scatter0": 8, "gather0": 10, "product0": 12, "tile0": 15}


def nt(first, second):
    return lax.dot_general(first, second, (((1,), (1,)), ((), ())), preferred_element_type=jnp.float32)


def nn(first, second):
    return jnp.dot(first, second, preferred_element_type=jnp.float32)


def kernel(
    a_ref, c_ref, w_ref, g_out,
    a_all, a_t, c_all, own_part, part_sum, part_send, part_recv,
    own, other, half, cs_send, cs_recv, zs_send, zs_recv, gram, prior, own_prod, ps_send, ps_recv,
    local_sem, a_ss, a_rs, c_ss, c_rs, p_ss, p_rs,
    o_ss, o_rs, q_ss, q_rs, cs_ss, cs_rs, zs_ss, zs_rs, ag_ss, ag_rs, fw_ss, fw_rs, ps_ss, ps_rs,
):
    d, x, c = lax.axis_index("dp"), lax.axis_index("row"), lax.axis_index("col")
    y_lo, z, y_hi, core = d // 8, d % 8, c // 2, c % 2
    y = y_hi * 2 + y_lo

    def dev(x2, y2, z2, core2):
        return ((y2 % 2) * 8 + z2, x2, (y2 // 2) * 2 + core2)

    left, right = dev((x + 3) % 4, y, z, core), dev((x + 1) % 4, y, z, core)
    sibling = dev(x, y, z, 1 - core)
    hops_y = [dev(x, (y + k) % 4, z, core) for k in range(1, 4)]
    hops_z = [dev(x, y, (z + k) % 8, core) for k in range(1, 8)]

    barrier = pltpu.get_barrier_semaphore()
    for target in [left, right, sibling] + hops_y:
        pl.semaphore_signal(barrier, inc=1, device_id=target)

    @pl.loop(1, 16)
    def _(k):
        pl.semaphore_signal(barrier, inc=1, device_id=((d + k) % 16, x, c))

    @pl.when(x != y)
    def _():
        for k in range(4):
            pl.semaphore_signal(barrier, inc=1, device_id=dev(y, k, z, core))

    def remote(src, dst, ss, rs, target):
        return pltpu.make_async_remote_copy(
            src_ref=src, dst_ref=dst, send_sem=ss, recv_sem=rs, device_id=target
        )

    c_rows = pl.ds(pl.multiple_of(x * 512, 512), 512)
    copy_c = pltpu.make_async_copy(c_ref, c_all.at[:, c_rows, :], local_sem.at[0])
    copy_c.start()
    my_cols = pl.ds(pl.multiple_of(y * 128, 128), 128)
    own[0, :, my_cols] = w_ref[...]

    def put_transposed(block, ref):
        cols = pl.ds(pl.multiple_of(block * 512, 512), 512)
        a_t[:, cols] = ref[...].T

    put_transposed(c, a_ref)
    pl.semaphore_wait(barrier, 24)

    def col_of(k):
        return pl.ds(pl.multiple_of(k * 128, 128), 128)

    def chunk_rows(j):
        return pl.ds(j * 256, 256)

    def core_rows(j, h):
        return pl.ds(pl.multiple_of(j * 256 + h * 128, 128), 128)

    def own_copy(k, j, hop):
        view = own.at[k, chunk_rows(j), my_cols]
        return remote(
            view, view, o_ss.at[k, j, hop], o_rs.at[k, j, y], dev(x, (y + hop) % 4, z, core)
        )

    def other_copy(k, j, hop):
        return remote(
            own.at[k, chunk_rows(j), my_cols], other.at[k, chunk_rows(j), my_cols],
            q_ss.at[k, j, hop], q_rs.at[k, j, y], dev((x + hop) % 4, x, z, core),
        )

    def send_tile(k, j):
        for hop in (2, 1, 3):
            other_copy(k, j, hop).start()
            own_copy(k, j, hop).start()

    def wait_own(k, j):
        for hop in range(1, 4):
            source = (y + hop) % 4
            view = own.at[k, chunk_rows(j), col_of(source)]
            remote(view, view, o_ss.at[k, j, hop], o_rs.at[k, j, source], sibling).wait_recv()

    def wait_tile(k):
        for j in range(2):
            wait_own(k, j)

        @pl.when(x != y)
        def _():
            for j in range(2):
                for source in range(4):
                    view = other.at[k, chunk_rows(j), col_of(source)]
                    remote(view, view, q_ss.at[k, j, 0], q_rs.at[k, j, source], sibling).wait_recv()

        @pl.when(x == y)
        def _():
            other[k] = own[k]

    def swap_copy(k, j):
        return remote(cs_send.at[k, j], cs_recv.at[k, j], cs_ss.at[k, j], cs_rs.at[k, j], sibling)

    def sym(k, pairs):
        wait_tile(k)

        def block(rows):
            total = None
            for first, second in pairs:
                term = nt(own[first, rows, :], other[second])
                total = term if total is None else total + term
            return total

        for j in range(2):
            cs_send[k, j] = block(core_rows(j, 1 - core)).astype(jnp.bfloat16)
            swap_copy(k, j).start()
        for j in range(2):
            half[k, j] = block(core_rows(j, core))

    def scatter_copy(k, j, hop):
        target = (z + hop) % 8
        return remote(
            zs_send.at[k, j, target], zs_recv.at[k, j, z], zs_ss.at[k, j, hop], zs_rs.at[k, j, z],
            dev(x, y, target, core),
        )

    def scatter(k):
        for j in range(2):
            swap_copy(k, j).wait_recv()
            total = half[k, j] + cs_recv[k, j].astype(jnp.float32)
            half[k, j] = total
            zs_send[k, j] = total.astype(jnp.bfloat16).reshape(8, 16, 512)
            for hop in (4, 3, 5, 2, 6, 1, 7):
                scatter_copy(k, j, hop).start()

    def piece_rows(j, owner):
        return pl.ds(pl.multiple_of(j * 256 + core * 128 + owner * 16, 16), 16)

    def gather_copy(k, j, hop):
        view = gram.at[k, piece_rows(j, z), :]
        return remote(
            view, view, ag_ss.at[k, j, hop], ag_rs.at[k, j, z], dev(x, y, (z + hop) % 8, core)
        )

    def gather(k):
        for j in range(2):
            total = half[k, j, pl.ds(pl.multiple_of(z * 16, 16), 16), :]
            for hop in range(1, 8):
                source = (z + hop) % 8
                view = zs_recv.at[k, j, source]
                remote(view, view, zs_ss.at[k, j, hop], zs_rs.at[k, j, source], sibling).wait_recv()
                total = total + zs_recv[k, j, source].astype(jnp.float32)
            gram[k, piece_rows(j, z), :] = total.astype(jnp.bfloat16)
            for hop in (4, 3, 5, 2, 6, 1, 7):
                gather_copy(k, j, hop).start()

    def half_copy(k, j):
        view = gram.at[k, core_rows(j, core), :]
        return remote(view, view, fw_ss.at[k, j], fw_rs.at[k, j], sibling)

    def swap(k, j):
        for hop in range(1, 8):
            source = (z + hop) % 8
            view = gram.at[k, piece_rows(j, source), :]
            remote(view, view, ag_ss.at[k, j, hop], ag_rs.at[k, j, source], sibling).wait_recv()
        half_copy(k, j).start()

    def product_copy(k, j, hop):
        target = (y + hop) % 4
        return remote(
            ps_send.at[k, target, chunk_rows(j)], ps_recv.at[k, y, chunk_rows(j)],
            ps_ss.at[k, j, hop], ps_rs.at[k, j, y], dev(x, target, z, core),
        )

    def product(k, j, pairs):
        view = gram.at[k, core_rows(j, 1 - core), :]
        remote(view, view, fw_ss.at[k, j], fw_rs.at[k, j], sibling).wait_recv()
        rows = chunk_rows(j)
        for hop in (2, 1, 3, 0):
            target = (y + hop) % 4
            cols = col_of(target)
            total = prior[rows, cols] if k >= 2 else None
            for matrix, panel in pairs:
                term = nn(gram[matrix, rows, :], other[panel, :, cols])
                total = term if total is None else total + term
            if hop:
                ps_send[k, target, rows] = total.astype(jnp.bfloat16)
                product_copy(k, j, hop).start()
            else:
                own_prod[k, rows, :] = total

    def prepare(matrix, panel):
        for j in range(2):
            prior[chunk_rows(j), :] = nn(gram[matrix, chunk_rows(j), :], other[panel])

    def swap_product(k, pairs):
        for j in range(2):
            swap(k, j)
            product(k, j, pairs)

    def result(k, j, tile):
        rows = chunk_rows(j)
        total = own_prod[k, rows, :]
        for hop in range(1, 4):
            source = (y + hop) % 4
            view = ps_recv.at[k, source, rows]
            remote(view, view, ps_ss.at[k, j, hop], ps_rs.at[k, j, source], sibling).wait_recv()
            total = total + ps_recv[k, source, rows].astype(jnp.float32)
        return 1.5 * own[tile, rows, my_cols].astype(jnp.float32) - 0.5 * total

    def finish_tile(k, tile, following):
        for j in range(2):
            own[following, chunk_rows(j), my_cols] = result(k, j, tile).astype(jnp.bfloat16)
            send_tile(following, j)

    def drain(k):
        for j in range(2):
            for hop in range(1, 4):
                own_copy(k, j, hop).wait_send()
                other_copy(k, j, hop).wait_send()
                product_copy(k, j, hop).wait_send()
            for hop in range(1, 8):
                scatter_copy(k, j, hop).wait_send()
                gather_copy(k, j, hop).wait_send()
            swap_copy(k, j).wait_send()
            half_copy(k, j).wait_send()

    far = dev(x, (y + 2) % 4, z, core)
    far_c = (c + 2) % 4
    a_far = remote(a_ref, a_all.at[c], a_ss.at[0], a_rs.at[c], far)
    a_sib = remote(a_ref, a_all.at[c], a_ss.at[1], a_rs.at[c], sibling)
    a_fwd = remote(a_all.at[far_c], a_all.at[far_c], a_ss.at[2], a_rs.at[far_c], sibling)
    sib_c = y_hi * 2 + 1 - core
    far_sib_c = (sib_c + 2) % 4

    def a_wait(block):
        view = a_all.at[block]
        remote(view, view, a_ss.at[0], a_rs.at[block], sibling).wait_recv()

    def chunk(i):
        return (d + 5 * (i + 1)) % 16

    def c_copy(i, way):
        view = c_all.at[chunk(i), c_rows, :]
        return remote(view, view, c_ss.at[i, way], c_rs.at[i, way], left if way else right)

    def rows_of(source):
        return pl.ds(pl.multiple_of(source * 512, 512), 512)

    def c_forward(i, way):
        source = (x + 3) % 4 if way == 0 else (x + 1) % 4
        view = c_all.at[chunk(i), rows_of(source), :]
        return remote(view, view, c_ss.at[i, 2], c_rs.at[i, 2], left if way else right)

    def c_wait(i, slot):
        view = c_all.at[chunk(i), rows_of(0), :]
        remote(view, view, c_ss.at[i, slot], c_rs.at[i, slot], sibling).wait_recv()

    def part_copy(i):
        a = chunk(i)
        return remote(part_send.at[a], part_recv.at[d], p_ss.at[a], p_rs.at[d], (a, x, c))

    copy_c.wait()
    c_copy(0, 0).start()
    c_copy(0, 1).start()
    send_tile(0, 0)
    send_tile(0, 1)
    a_far.start()
    a_sib.start()
    for i in range(1, LOOKAHEAD):
        c_copy(i, 0).start()
        c_copy(i, 1).start()
    a_wait(sib_c)
    put_transposed(sib_c, a_all.at[sib_c])

    stages = {
        "sym0": lambda: sym(0, [(0, 0)]),
        "scatter0": lambda: scatter(0),
        "gather0": lambda: gather(0),
        "product0": lambda: swap_product(0, [(0, 0)]),
        "tile0": lambda: finish_tile(0, 0, 1),
        "sym1": lambda: sym(1, [(1, 1)]),
    }

    def source_of(k):
        return (d + 80 - 5 * (k + 1)) % 16

    def part_wait(k):
        source = source_of(k)
        view = part_recv.at[source]
        remote(view, view, p_ss.at[source], p_rs.at[source], sibling).wait_recv()

    part_sum[...] = jnp.zeros_like(part_sum)

    @pl.loop(0, 17)
    def _(i):
        @pl.when(i + LOOKAHEAD < 16)
        def _():
            c_copy(i + LOOKAHEAD, 0).start()
            c_copy(i + LOOKAHEAD, 1).start()

        @pl.when(i < 16)
        def _():
            c_wait(i, 0)
            c_wait(i, 1)

            @pl.when(i % 2 == 0)
            def _():
                c_forward(i, 0).start()

            @pl.when(i % 2 == 1)
            def _():
                c_forward(i, 1).start()

        @pl.when(i == 0)
        def _():
            a_wait(far_c)
            a_fwd.start()
            put_transposed(far_c, a_all.at[far_c])
            a_wait(far_sib_c)
            put_transposed(far_sib_c, a_all.at[far_sib_c])

        @pl.when(i > 0)
        def _():
            c_wait(i - 1, 2)
            a = chunk(i - 1)
            block = nn(a_t[...], c_all[a])

            @pl.when(i < 16)
            def _():
                part_send[a] = block.astype(jnp.bfloat16)
                part_copy(i - 1).start()

            @pl.when(i == 16)
            def _():
                own_part[...] = block

        @pl.when(i > LAG)
        def _():
            part_wait(i - LAG - 1)
            part_sum[...] += part_recv[source_of(i - LAG - 1)].astype(jnp.float32)

        for name, place in PLACES.items():
            if place < 17:
                @pl.when(i == place)
                def _(name=name):
                    stages[name]()


    for k in range(16 - LAG, 15):
        part_wait(k)

    for j in range(2):
        @pl.loop(j * 4, j * 4 + 4)
        def _(m):
            rows = pl.ds(pl.multiple_of(m * 64, 64), 64)
            total = own_part[rows, :] + part_sum[rows, :]
            for k in range(16 - LAG, 15):
                total = total + part_recv[source_of(k), rows, :].astype(jnp.float32)
            own[2, rows, my_cols] = total.astype(jnp.bfloat16)

        send_tile(2, j)

    sym(1, [(1, 1)])
    scatter(1)
    for copy in (a_far, a_sib, a_fwd):
        copy.wait_send()

    @pl.loop(0, 16)
    def _(i):
        c_copy(i, 0).wait_send()
        c_copy(i, 1).wait_send()
        c_forward(i, 0).wait_send()

    @pl.loop(0, 15)
    def _(i):
        part_copy(i).wait_send()

    sym(2, [(2, 1), (1, 2)])
    gather(1)
    scatter(2)
    drain(0)
    swap(1, 0)
    swap(1, 1)
    gather(2)
    product(1, 0, [(1, 1)])
    product(1, 1, [(1, 1)])
    prepare(1, 2)
    swap_product(2, [(2, 1)])
    finish_tile(2, 2, 3)
    for j in range(2):
        g_out[chunk_rows(j), pl.ds(128, 128)] = result(1, j, 1)
    drain(1)
    drain(2)
    sym(3, [(3, 0), (0, 3)])
    scatter(3)
    gather(3)
    prepare(0, 3)
    swap_product(3, [(3, 0)])
    for j in range(2):
        g_out[chunk_rows(j), pl.ds(0, 128)] = result(3, j, 3)
    drain(3)


def body(activations, cotangent, weight):
    chunks = cotangent.transpose(1, 0, 2)
    bf16, f32 = jnp.bfloat16, jnp.float32
    sems = [
        (1,), (3,), (4,), (16, 3), (16, 3), (16,), (16,),
        (4, 2, 4), (4, 2, 4), (4, 2, 4), (4, 2, 4), (4, 2), (4, 2), (4, 2, 8), (4, 2, 8), (4, 2, 8), (4, 2, 8),
        (4, 2), (4, 2), (4, 2, 4), (4, 2, 4),
    ]
    buffers = [
        ((4, 512, 512), bf16), ((512, 2048), bf16), ((16, 2048, 128), bf16), ((512, 128), f32), ((512, 128), f32),
        ((16, 512, 128), bf16), ((16, 512, 128), bf16),
        ((4, 512, 512), bf16), ((4, 512, 512), bf16), ((4, 2, 128, 512), f32), ((4, 2, 128, 512), bf16),
        ((4, 2, 128, 512), bf16), ((4, 2, 8, 16, 512), bf16), ((4, 2, 8, 16, 512), bf16), ((4, 512, 512), bf16),
        ((512, 512), f32), ((4, 512, 128), f32), ((4, 4, 512, 128), bf16), ((4, 4, 512, 128), bf16),
    ]
    vmem = pl.BlockSpec(memory_space=pltpu.VMEM)
    both = pl.pallas_call(
        kernel,
        out_shape=jax.ShapeDtypeStruct((512, 256), f32),
        in_specs=[vmem, pl.BlockSpec(memory_space=pl.ANY), vmem],
        out_specs=vmem,
        scratch_shapes=[pltpu.VMEM(s, t) for s, t in buffers] + [pltpu.SemaphoreType.DMA(s) for s in sems],
        compiler_params=pltpu.CompilerParams(
            collective_id=0, has_side_effects=True, vmem_limit_bytes=56 * 2**20
        ),
    )(activations, chunks, weight)
    return both[:, 128:].astype(bf16), both[:, :128]


def solution(mesh):
    placed = (P(("dp", "col"), "row"), P(("dp", "row"), None, "col"), P("row", ("dp", "col")))
    return jax.shard_map(
        body,
        mesh=mesh,
        in_specs=placed,
        out_specs=(P("row", ("dp", "col")), P("row", ("dp", "col"))),
        check_vma=False,
    )
```
